256 devices in a mesh: cluster: 32 (over x, y, core), dp: 8 (over z).
Axes of the slice: x: 4, y: 4, z: 8, core: 2. Of those that a mesh axis runs over, the one named last changes fastest.
Arguments:
- hidden_states: bfloat16 [32768, 768], P(('cluster', 'dp')), may hold values from -1.5 to 1.5
- ln_gain: float32 [768], replicated, may hold values from 0.5 to 1.5
- beam_ids: int32 [32768, 8], P(('cluster', 'dp')), may hold values from 0 to 31, all different within a row; in each aligned block of 128 rows (0 to 127, 128 to 255, ...) at most 64 rows name the same one
- positive_ids: int32 [32768, 8], P(('cluster', 'dp')), may hold values from 0 to 4095
- cluster_sizes: int32 [32], P('cluster'), may hold values from 128 to 512
- head_rows: float32 [32, 512, 768], P('cluster'), may hold values from -0.21875 to 0.21875
- first_moment: float32 [32, 512, 768], P('cluster'), may hold values from -3 to 3
- second_moment: float32 [32, 512, 768], P('cluster'), may hold values from 0.01 to 1
Outputs:
- new_head: float32 [32, 512, 768], P('cluster')
- new_first: float32 [32, 512, 768], P('cluster')
- new_second: float32 [32, 512, 768], P('cluster')
- input_grad: bfloat16 [32768, 768], P(('cluster', 'dp'))
- gain_grad: float32 [768], replicated
The draws below stay inside these ranges and needn't reach their ends.
Inputs may be any that keep to these rules, and one draw needn't show every extreme that they name: `beam_ids`: each row names 8 different clusters. Within the rows of one device no cluster is named by more than 64 rows, and in every draw some cluster is named by exactly 64 rows of some device.
All inputs are finite; a program needn't handle non-finite values.
Results may differ from the reference program's by a relative error of at most 0.025.
Values may be sent and summed in bfloat16 or wider, within the bound.
A program may use at most 128 MiB of HBM per device.

```python
import math
import jax
import jax.numpy as jnp
import numpy as np
from jax import lax

D = 768
CL = 512
BEAM = 8
POS = 8
INST_DEV = 128
NCLUS = 32
INSTANCES = 32768
CAP = 64
N_CLUSTER = 32
N_DP = 8


def plant(entries, key, smallest, largest):
    place = [jax.random.randint(jax.random.fold_in(key, axis), (), 0, length) for axis, length in enumerate(entries.shape)]
    widest = entries.shape.index(max(entries.shape))
    next_to = place[:widest] + [(place[widest] + 1) % entries.shape[widest]] + place[widest + 1:]
    return entries.at[tuple(place)].set(smallest).at[tuple(next_to)].set(largest)


def level_of(rng, shape, shards, smallest, top_value):
    gain, own = 1.0, jax.random.fold_in(rng, 6)
    for axis_at, blocks in shards:
        draws = jnp.exp(jax.random.uniform(jax.random.fold_in(own, axis_at), (blocks,), jnp.float32, smallest / len(shards), top_value / len(shards)))
        gain = gain * jnp.repeat(draws, shape[axis_at] // blocks).reshape([-1 if axis == axis_at else 1 for axis in range(len(shape))])
    return gain


def deal_out(own_key, own, number, rows, amount, top, reach, skew):
    sequence = jax.random.permutation(own_key, amount)
    crowded, common = portions_of(amount, rows * top, reach, skew, True), portions_of(amount, rows * top, reach, skew, False)
    places = jnp.arange(amount)

    def named(lengths, turn):
        used = int((lengths > 0).sum())
        fixed = max(1, used // 4)
        passed = fixed + (places - fixed + turn * (used - fixed)) % max(1, amount - fixed)
        return jnp.zeros((amount,), jnp.int32).at[sequence[jnp.where(places < fixed, places, passed)]].set(jnp.asarray(lengths, jnp.int32))

    lengths = jnp.where(number % 4 == 0, named(crowded, number // 4), named(common, number - number // 4 - 1))
    mixed = jax.random.permutation(jax.random.fold_in(own, 3), amount)
    donor, receiver = mixed[0:amount // 2 * 2:2], mixed[1:amount // 2 * 2:2]
    room = jnp.minimum(lengths[donor] - 1, reach - lengths[receiver]) // 2
    room = jnp.where((donor == sequence[0]) | (receiver == sequence[0]) | (lengths[receiver] == 0), 0, jnp.maximum(room, 0))
    passed = jax.random.randint(jax.random.fold_in(own, 4), (amount // 2,), 0, 1 << 20) % (room + 1)
    lengths = lengths.at[donor].add(-passed).at[receiver].add(passed)
    members = jnp.searchsorted(jnp.cumsum(lengths), jnp.arange(rows * top), side="right").astype(jnp.int32)
    listing = members.reshape(top, rows).T
    listing = listing[jax.random.permutation(jax.random.fold_in(own, 1), rows)]
    turn = jax.random.randint(jax.random.fold_in(own, 2), (rows, 1), 0, top)
    return jnp.take_along_axis(listing, (jnp.arange(top)[None, :] + turn) % top, axis=1)


def portions_of(count, total, limit, skew, full):
    portions = [(1 << 20) // math.isqrt(standing ** skew) + 1 for standing in range(1, count + 1)]
    largest = limit if full else min(limit, max(-(-total // count), total * portions[0] // sum(portions)))
    least = 1 if total - largest >= count - 1 else 0
    given, spare = [largest] + [least] * (count - 1), total - largest - least * (count - 1)
    while spare > 0:
        candidates = [i for i in range(1, count) if given[i] < largest] or [i for i in range(1, count) if given[i] < limit]
        mass, remaining = sum([portions[i] for i in candidates]), spare
        for i in candidates:
            more = min(limit - given[i], max(1, remaining * portions[i] // mass), spare)
            given[i] = given[i] + more
            spare = spare - more
    return np.array(given)


def scatter_about(key, shape, scale, bound, split=(), kind=jnp.bfloat16):
    entries = jax.random.normal(key, shape, jnp.float32) * scale
    if len(split) > 0:
        entries = level_of(key, shape, split, -0.22, 0.18) * entries
    return jnp.clip(entries, min=-bound, max=bound).astype(kind)


def setup_inputs(seed: int = 0) -> dict:
    seeds = jax.random.split(jax.random.key(seed), 9)
    hidden_states = scatter_about(seeds[0], (INSTANCES, D), 0.25, 1.5, ((0, 256),))
    ln_gain = jnp.clip(1.0 + 0.1 * jax.random.normal(seeds[1], (D,), jnp.float32), 0.5, 1.5)
    beam_ids_keys = jax.random.split(jax.random.fold_in(seeds[2], 1), INSTANCES // INST_DEV)
    beam_ids_turns = jax.random.permutation(jax.random.fold_in(seeds[2], 3), INSTANCES // INST_DEV)
    beam_ids = jax.vmap(lambda own, number: deal_out(jax.random.fold_in(seeds[2], 2), own, number, INST_DEV, NCLUS, BEAM, CAP, 2))(beam_ids_keys, beam_ids_turns).reshape((INSTANCES, BEAM))
    positive_ids = plant(jax.random.randint(seeds[3], (INSTANCES, POS), 0, BEAM * CL), jax.random.fold_in(seeds[3], 1), 0, (BEAM * CL) - 1).astype(jnp.int32)
    cluster_sizes = plant(jax.random.randint(seeds[4], (NCLUS,), CL // 4, CL + 1), jax.random.fold_in(seeds[4], 1), CL // 4, CL).astype(jnp.int32)
    head_rows = scatter_about(seeds[5], (NCLUS, CL, D), D ** -0.5, 0.21875, ((0, 32),), jnp.float32)
    first_moment = scatter_about(seeds[6], (NCLUS, CL, D), 0.5, 3.0, ((0, 32),), jnp.float32)
    second_moment = jnp.clip(jnp.exp(math.log(1.0) - 4.6051702 * jax.random.uniform(seeds[7], (NCLUS, CL, D), jnp.float32) ** level_of(seeds[7], (NCLUS, CL, D), ((0, 32),), -0.2, 0.2)), 0.01, 1.0)
    return {"hidden_states": hidden_states, "ln_gain": ln_gain, "beam_ids": beam_ids, "positive_ids": positive_ids, "cluster_sizes": cluster_sizes, "head_rows": head_rows, "first_moment": first_moment, "second_moment": second_moment}


norm_eps = 1e-05
learn_rate = 0.01
first_decay = 0.9
second_decay = 0.999
adam_eps = 1e-08
second_fix = 0.632304575226

def normalize(hidden_states, ln_gain):
    values = hidden_states.astype(jnp.float32)
    center = lax.optimization_barrier(jnp.mean(values, axis=1, keepdims=True))
    spread = lax.optimization_barrier(jnp.mean(jnp.square(values - center), axis=1, keepdims=True))
    inverse = lax.rsqrt(spread + norm_eps)
    normed = (values - center) * inverse
    return (normed, inverse, (normed * ln_gain).astype(jnp.bfloat16))

def norm_backward(emb_grad, normed, inverse, ln_gain):
    scaled = emb_grad * ln_gain
    first_mean = lax.optimization_barrier(jnp.mean(scaled, axis=1, keepdims=True))
    second_mean = lax.optimization_barrier(jnp.mean(scaled * normed, axis=1, keepdims=True))
    return ((scaled - first_mean - normed * second_mean) * inverse).astype(jnp.bfloat16)

def adam_update(head_rows, first_moment, second_moment, head_grad):
    new_first = first_decay * first_moment + (1.0 - first_decay) * head_grad
    new_second = second_decay * second_moment + (1.0 - second_decay) * head_grad * head_grad
    step_size = new_first / (jnp.sqrt(new_second / second_fix) + adam_eps)
    return (head_rows - learn_rate * step_size, new_first, new_second)

def reference(hidden_states, ln_gain, beam_ids, positive_ids, cluster_sizes, head_rows, first_moment, second_moment):
    normed, inverse, embedded = normalize(hidden_states, ln_gain)
    total_rows = embedded.shape[0]
    width = embedded.shape[1]
    padded_emb = jnp.concatenate([embedded, jnp.zeros((1, width), embedded.dtype)], axis=0)
    label_iota = jnp.arange(CL, dtype=jnp.int32)
    beam_iota = jnp.arange(BEAM, dtype=jnp.int32)
    live_total = N_DP * N_CLUSTER * CAP

    def per_cluster(running, cluster):
        match = beam_ids == cluster
        chosen = jnp.any(match, axis=1)
        position = lax.optimization_barrier(jnp.sum(jnp.where(match, beam_iota, 0), axis=1)).astype(jnp.int32)
        picked = jnp.nonzero(chosen, size=live_total, fill_value=total_rows)[0].astype(jnp.int32)
        rows_in = padded_emb[picked]
        safe_rows = jnp.minimum(picked, total_rows - 1)
        offset = positive_ids[safe_rows] - position[safe_rows][:, None] * CL
        weights = lax.dynamic_index_in_dim(head_rows, cluster, 0, keepdims=False).astype(jnp.bfloat16)
        logits = jnp.dot(rows_in, weights.T, preferred_element_type=jnp.float32)
        target = jnp.any(offset[:, :, None] == label_iota, axis=1).astype(jnp.float32)
        size_here = lax.dynamic_index_in_dim(cluster_sizes, cluster, 0, keepdims=False)
        live = (label_iota[None, :] < size_here) & (picked < total_rows)[:, None]
        slope = (jnp.where(live, jax.nn.sigmoid(logits) - target, 0.0) / BEAM).astype(jnp.bfloat16)
        grad_block = lax.dot_general(slope, rows_in, (((0,), (0,)), ((), ())), preferred_element_type=jnp.float32)
        returned = jnp.dot(slope, weights, preferred_element_type=jnp.float32).astype(jnp.bfloat16)
        running = running.at[picked].add(returned.astype(jnp.float32))
        return (running, grad_block)
    start_acc = jnp.zeros((total_rows + 1, width), jnp.float32)
    emb_acc, head_grad = lax.scan(per_cluster, start_acc, jnp.arange(NCLUS, dtype=jnp.int32))
    emb_grad = emb_acc[:total_rows]
    gain_grad = lax.optimization_barrier(jnp.sum(emb_grad * normed, axis=0))
    input_grad = norm_backward(emb_grad, normed, inverse, ln_gain)
    new_head, new_first, new_second = adam_update(head_rows, first_moment, second_moment, head_grad)
    return (new_head, new_first, new_second, input_grad, gain_grad)
```

```python
import functools

import jax
import jax.numpy as jnp
from jax import lax
from jax.experimental import pallas as pl
from jax.experimental.pallas import tpu as pltpu
from jax.sharding import PartitionSpec as P

MESH = pl.DeviceIdType.MESH
F32 = jnp.float32
BF16 = jnp.bfloat16

norm_eps = 1e-05
learn_rate = 0.01
first_decay = 0.9
second_decay = 0.999
adam_eps = 1e-08
second_fix = 0.632304575226

SIDE = 4
PLANE = 32
CHIPS = (
    (0, 0), (1, 0), (0, 1), (3, 0), (0, 3), (2, 0), (0, 2), (1, 1),
    (3, 3), (1, 3), (3, 1), (2, 1), (1, 2), (2, 3), (3, 2), (2, 2),
)


def table_at(values, at):
    half = len(values) // 2
    low = sum(v * 4**i for i, v in enumerate(values[:half]))
    high = sum(v * 4**i for i, v in enumerate(values[half:]))
    above = at // half
    word = low + above * (high - low)
    return lax.rem(lax.shift_right_logical(word, 2 * lax.rem(at, half)), 4)


def kernel(
    hid_ref, gain_ref, ids_ref, size_ref, head_ref,
    hg_ref, igrad_ref, ggrad_ref,
    emb, ids, wh, wt, hg, part, from_core, half_in, quart_in, half_in2, quart_in2,
    hgb, hgf, zq, zh, gplane, gz, egrad,
    ids_sem, ag_send, ag_recv, core_recv,
    rs_send, rs_core, rs_h, rs_q, rs_h2, rs_q2,
    z_send, z_q, z_h, zg_send, zg, g_sem,
):
    c = lax.axis_index("cluster")
    z = lax.axis_index("dp")
    depth = lax.axis_size("dp")
    rows, width = hid_ref.shape
    labels = head_ref.shape[0]
    beam = 8
    x, y, k = c // (2 * SIDE), lax.rem(c // 2, SIDE), lax.rem(c, 2)
    sibling = (c + 1 - 2 * k, z)

    def chip(dx, dy):
        return lax.rem(x + dx, SIDE) * SIDE + lax.rem(y + dy, SIDE)

    def chip_t(t, du, dv):
        return chip(du, dv) if t == 0 else chip(dv, du)

    def peer_t(t, du, dv):
        return (2 * chip_t(t, du, dv) + k, z)

    def copy(src, dst, send, recv, dev):
        return pltpu.make_async_remote_copy(
            src_ref=src, dst_ref=dst, send_sem=send, recv_sem=recv, device_id=dev, device_id_type=MESH
        )

    def arrived(dst, recv):
        copy(dst, dst, recv, recv, sibling).wait_recv()

    def sent(src, send):
        copy(src, src, send, send, sibling).wait_send()

    barrier = pltpu.get_barrier_semaphore()

    def greet(i, _):
        pl.semaphore_signal(barrier, inc=1, device_id=(lax.rem(c + i, PLANE), z), device_id_type=MESH)
        return _

    def greet_z(i, _):
        pl.semaphore_signal(barrier, inc=1, device_id=(c, lax.rem(z + i, depth)), device_id_type=MESH)
        return _

    lax.fori_loop(1, PLANE, greet, 0)
    lax.fori_loop(1, depth, greet_z, 0)

    values = hid_ref[...].astype(F32)
    center = jnp.mean(values, axis=1, keepdims=True)
    spread = jnp.mean(jnp.square(values - center), axis=1, keepdims=True)
    normed = (values - center) * lax.rsqrt(spread + norm_eps)
    emb[c] = (normed * gain_ref[...]).astype(BF16)
    ids[c] = ids_ref[...]
    pl.semaphore_wait(barrier, PLANE - 1 + depth - 1)

    half, quart = rows // 2, rows // 4

    def event(dx, dy):
        src = 2 * chip(dx, dy) + k
        for t in range(2):
            du, dv = (dx, dy) if t == 0 else (dy, dx)
            whole = emb.at[src, pl.ds(t * half, half)]
            q = [emb.at[src, pl.ds(t * half + i * quart, quart)] for i in range(2)]
            if (dx, dy) != (0, 0):
                arrived(whole, ag_recv.at[t, du, dv])

            def push(ref, tu, tv, t=t, du=du, dv=dv):
                there = ag_recv.at[t, (du - tu) % SIDE, (dv - tv) % SIDE]
                copy(ref, ref, ag_send, there, peer_t(t, tu % SIDE, tv % SIDE)).start()

            if dv == 0:
                if du == 0:
                    push(whole, 1, 0)
                    push(whole, -1, 0)
                elif du == 3:
                    push(q[0], 1, 0)
                elif du == 1:
                    push(q[1], -1, 0)
                push(whole, 0, 1)
                push(whole, 0, -1)
            elif dv == 3:
                push(q[0], 0, 1)
            elif dv == 1:
                push(q[1], 0, -1)
        copy(emb.at[src], emb.at[src], ag_send, core_recv.at[dx, dy], sibling).start()

    def send_ids(i, _):
        copy(ids.at[c], ids.at[c], ids_sem.at[0], ids_sem.at[1], (lax.rem(c + i, PLANE), z)).start()
        return _

    event(0, 0)
    lax.fori_loop(1, PLANE, send_ids, 0)

    wh[...] = (head_ref[...].astype(BF16) * 0.5).astype(BF16)
    for i in range(width // 128):
        cols = pl.ds(i * 128, 128)
        wt[cols, :] = head_ref[:, cols].T.astype(BF16)
    hg[...] = jnp.zeros_like(hg)
    size = size_ref[0]
    arrived(ids.at[pl.ds(0, PLANE - 1)], ids_sem.at[1])

    def compute(at):
        dx, dy = table_at([p[0] for p in CHIPS], at), table_at([p[1] for p in CHIPS], at)
        ch = chip(dx, dy)
        arrived(emb.at[2 * ch + 1 - k], core_recv.at[dx, dy])
        block = emb[pl.ds(2 * ch, 2)].reshape(2 * rows, width)
        label, limit = [], []
        for s in range(2):
            own = ids[2 * ch + s].astype(jnp.int32)
            match = own[0:beam] == c
            place = lax.broadcasted_iota(jnp.int32, (beam, rows), 0)
            place = jnp.sum(jnp.where(match, place, 0), axis=0, keepdims=True)
            chosen = jnp.max(jnp.where(match, 1, 0), axis=0, keepdims=True)
            label.append(own[beam:] - place * labels)
            limit.append(chosen * size)
        label = jnp.concatenate(label, axis=1)
        limit = jnp.concatenate(limit, axis=1)
        logits = lax.dot_general(wh[...], block, (((1,), (1,)), ((), ())), preferred_element_type=F32)
        slot = lax.broadcasted_iota(jnp.int32, (labels, 2 * rows), 0)
        hit = label[0:1] == slot
        for p in range(1, label.shape[0]):
            hit = hit | (label[p : p + 1] == slot)
        step = 0.5 / beam
        slope = step * jnp.tanh(logits) + jnp.where(hit, -step, step)
        slope = jnp.where(slot < limit, slope, 0.0).astype(BF16)
        hg[...] += jnp.dot(slope, block, preferred_element_type=F32)
        back = jnp.dot(wt[...], slope, preferred_element_type=F32).astype(BF16)
        part[2 * ch] = back[:, :rows]
        part[2 * ch + 1] = back[:, rows:]
        there = 2 * ch + 1 - k
        copy(part.at[there], from_core.at[ch], rs_send, rs_core.at[dx, dy], sibling).start()

    def join(at):
        dx, dy = table_at([p[0] for p in CHIPS], at), table_at([p[1] for p in CHIPS], at)
        ch = chip(dx, dy)
        arrived(from_core.at[ch], rs_core.at[dx, dy])
        part[2 * ch + k] += from_core[ch]

    count = len(CHIPS)

    def turn(e, _):
        for i in range(1, count):
            pl.when(e == i)(functools.partial(event, *CHIPS[i]))

        @pl.when((e >= 1) & (e <= count))
        def _compute():
            compute(e - 1)

        @pl.when(e >= 2)
        def _join():
            join(e - 2)

        return _

    lax.fori_loop(1, count + 2, turn, 0)

    piece = labels // depth
    far = depth // 2

    def at_z(i):
        return lax.rem(z + i + depth, depth)

    def rows_z(i, lo=0, n=piece):
        return pl.ds(pl.multiple_of(at_z(i) * piece + lo, piece // 2), n)

    hgb[...] = hg[...].astype(BF16)

    def z_first():
        for s in range(2):
            lo = s * (piece // 2)
            src = hgb.at[rows_z(far, lo, piece // 2)]
            copy(src, zq.at[s], z_send, z_q.at[s], (c, at_z(1 - 2 * s))).start()

    def z_next(i):
        for s in range(2):
            way = 1 - 2 * s
            own = rows_z(way * (far - 1 - i))
            if i == 0:
                arrived(zq.at[s], z_q.at[s])
                mid = rows_z(way * (far - 1), s * (piece // 2), piece // 2)
                hgb[mid] += zq[s]
            else:
                arrived(zh.at[s, i - 1], z_h.at[s, i - 1])
                hgb[own] += zh[s, i - 1]
            copy(hgb.at[own], zh.at[s, i], z_send, z_h.at[s, i], (c, at_z(way))).start()

    def z_last():
        total = hgb[rows_z(0)].astype(F32)
        for s in range(2):
            arrived(zh.at[s, far - 2], z_h.at[s, far - 2])
            total += zh[s, far - 2].astype(F32)
        hgf[rows_z(0)] = total.astype(BF16)
        for s in range(2):
            own = hgf.at[rows_z(0)]
            copy(own, own, zg_send, zg.at[s, 0], (c, at_z(1 - 2 * s))).start()

    def z_spread(i):
        for s in range(2):
            way = 1 - 2 * s
            own = hgf.at[rows_z(-way * i)]
            arrived(own, zg.at[s, i - 1])
            if i == far - 1:
                own = hgf.at[rows_z(-way * i, s * (piece // 2), piece // 2)]
            copy(own, own, zg_send, zg.at[s, i], (c, at_z(way))).start()

    def z_end():
        for s in range(2):
            arrived(hgf.at[rows_z(far, s * (piece // 2), piece // 2)], zg.at[s, far - 1])

    fh, fq = width // 2, width // 4

    def feats(t, lo, n):
        return pl.ds(t * fh + lo, n)

    def dest(t, du, dv):
        return 2 * chip_t(t, du % SIDE, dv % SIDE) + k

    def v_first(t, du):
        for s in range(2):
            src = part.at[dest(t, du, 2), feats(t, s * fq, fq)]
            copy(src, quart_in.at[t, du, s], rs_send, rs_q.at[t, du, s], peer_t(t, 0, (1, 3)[s])).start()

    def v_next(t, du):
        for s in range(2):
            arrived(quart_in.at[t, du, s], rs_q.at[t, du, s])
            to = dest(t, du, (1, 3)[s])
            part[to, feats(t, s * fq, fq)] += quart_in[t, du, s]
            src = part.at[to, feats(t, 0, fh)]
            copy(src, half_in.at[t, du, s], rs_send, rs_h.at[t, du, s], peer_t(t, 0, (1, 3)[s])).start()

    def v_last(t, du):
        to = dest(t, du, 0)
        for s in range(2):
            arrived(half_in.at[t, du, s], rs_h.at[t, du, s])
        total = part[to, feats(t, 0, fh)].astype(F32)
        total += half_in[t, du, 0].astype(F32) + half_in[t, du, 1].astype(F32)
        part[to, feats(t, 0, fh)] = total.astype(BF16)

    def u_first(t):
        for s in range(2):
            src = part.at[dest(t, 2, 0), feats(t, s * fq, fq)]
            copy(src, quart_in2.at[t, s], rs_send, rs_q2.at[t, s], peer_t(t, (1, 3)[s], 0)).start()

    def u_next(t):
        for s in range(2):
            arrived(quart_in2.at[t, s], rs_q2.at[t, s])
            to = dest(t, (1, 3)[s], 0)
            part[to, feats(t, s * fq, fq)] += quart_in2[t, s]
            src = part.at[to, feats(t, 0, fh)]
            copy(src, half_in2.at[t, s], rs_send, rs_h2.at[t, s], peer_t(t, (1, 3)[s], 0)).start()

    def u_last(t):
        for s in range(2):
            arrived(half_in2.at[t, s], rs_h2.at[t, s])
        total = part[c, feats(t, 0, fh)].astype(F32)
        total += half_in2[t, 0].astype(F32) + half_in2[t, 1].astype(F32)
        egrad[feats(t, 0, fh), :] = total

    def g_first():
        total = jnp.sum(wh[...].astype(F32) * hg[...], axis=0, keepdims=True)
        gplane[c] = total * 2.0

        def send(i, _):
            to = (lax.rem(c + i, PLANE), z)
            copy(gplane.at[c], gplane.at[c], g_sem.at[0], g_sem.at[1], to).start()
            return _

        lax.fori_loop(1, PLANE, send, 0)

    def g_next():
        arrived(gplane.at[pl.ds(0, PLANE - 1)], g_sem.at[1])
        gz[z] = jnp.sum(gplane[...], axis=0)

        def send(i, _):
            copy(gz.at[z], gz.at[z], g_sem.at[2], g_sem.at[3], (c, at_z(i))).start()
            return _

        lax.fori_loop(1, depth, send, 0)

    def g_last():
        arrived(gz.at[pl.ds(0, depth - 1)], g_sem.at[3])
        ggrad_ref[...] = jnp.sum(gz[...], axis=0) / gain_ref[...]

    z_first()
    for du in (2, 1, 3, 0):
        for t in range(2):
            v_first(t, du)
    g_first()
    z_next(0)
    for t in range(2):
        v_next(t, 2)
    z_next(1)
    for du in (1, 3):
        for t in range(2):
            v_next(t, du)
    z_next(2)
    for t in range(2):
        v_next(t, 0)
    for t in range(2):
        v_last(t, 2)
        u_first(t)
    z_last()
    for du in (1, 3):
        for t in range(2):
            v_last(t, du)
    for t in range(2):
        u_next(t)
    z_spread(1)
    g_next()
    for t in range(2):
        v_last(t, 0)
    z_spread(2)
    for t in range(2):
        u_last(t)
    z_spread(3)

    emb_grad = egrad[...].T
    values = hid_ref[...].astype(F32)
    center = jnp.mean(values, axis=1, keepdims=True)
    spread = jnp.mean(jnp.square(values - center), axis=1, keepdims=True)
    inverse = lax.rsqrt(spread + norm_eps)
    normed = (values - center) * inverse
    scaled = emb_grad * gain_ref[...]
    first_mean = jnp.mean(scaled, axis=1, keepdims=True)
    second_mean = jnp.mean(scaled * normed, axis=1, keepdims=True)
    igrad_ref[...] = ((scaled - first_mean - normed * second_mean) * inverse).astype(BF16)

    g_last()
    z_end()
    hg_ref[...] = hgf[...]

    sent(emb.at[pl.ds(0, PLANE - 1)], ag_send)
    sent(part.at[pl.ds(0, PLANE - 1)], rs_send)
    sent(ids.at[pl.ds(0, PLANE - 1)], ids_sem.at[0])
    sent(gplane.at[pl.ds(0, PLANE - 1)], g_sem.at[0])
    sent(gz.at[pl.ds(0, depth - 1)], g_sem.at[2])
    sent(hgb.at[pl.ds(0, labels - piece)], z_send)
    sent(hgf.at[pl.ds(0, labels - piece)], zg_send)


def adam_update(head_rows, first_moment, second_moment, head_grad):
    new_first = first_decay * first_moment + (1.0 - first_decay) * head_grad
    new_second = second_decay * second_moment + (1.0 - second_decay) * head_grad * head_grad
    step_size = new_first / (jnp.sqrt(new_second / second_fix) + adam_eps)
    return (head_rows - learn_rate * step_size, new_first, new_second)


def shards(
    hidden_states,
    ln_gain,
    beam_ids,
    positive_ids,
    cluster_sizes,
    head_rows,
    first_moment,
    second_moment,
):
    rows, width = hidden_states.shape
    labels = head_rows.shape[1]
    depth = lax.axis_size("dp")
    ids = jnp.concatenate([beam_ids.T, positive_ids.T], axis=0).astype(jnp.int16)
    vmem = pl.BlockSpec(memory_space=pltpu.VMEM)
    smem = pl.BlockSpec(memory_space=pltpu.SMEM)
    fh, fq, piece, far = width // 2, width // 4, labels // depth, depth // 2
    dma = pltpu.SemaphoreType.DMA
    head_grad, input_grad, gain_grad = pl.pallas_call(
        kernel,
        out_shape=(
            jax.ShapeDtypeStruct((labels, width), BF16),
            jax.ShapeDtypeStruct((rows, width), BF16),
            jax.ShapeDtypeStruct((1, width), F32),
        ),
        in_specs=[vmem, vmem, vmem, smem, vmem],
        out_specs=(vmem, vmem, vmem),
        scratch_shapes=[
            pltpu.VMEM((PLANE, rows, width), BF16),
            pltpu.VMEM((PLANE, 16, rows), jnp.int16),
            pltpu.VMEM((labels, width), BF16),
            pltpu.VMEM((width, labels), BF16),
            pltpu.VMEM((labels, width), F32),
            pltpu.VMEM((PLANE, width, rows), BF16),
            pltpu.VMEM((PLANE // 2, width, rows), BF16),
            pltpu.VMEM((2, SIDE, 2, fh, rows), BF16),
            pltpu.VMEM((2, SIDE, 2, fq, rows), BF16),
            pltpu.VMEM((2, 2, fh, rows), BF16),
            pltpu.VMEM((2, 2, fq, rows), BF16),
            pltpu.VMEM((labels, width), BF16),
            pltpu.VMEM((labels, width), BF16),
            pltpu.VMEM((2, piece // 2, width), BF16),
            pltpu.VMEM((2, far - 1, piece, width), BF16),
            pltpu.VMEM((PLANE, 1, width), F32),
            pltpu.VMEM((depth, 1, width), F32),
            pltpu.VMEM((width, rows), F32),
            dma((2,)),
            dma,
            dma((2, SIDE, SIDE)),
            dma((SIDE, SIDE)),
            dma,
            dma((SIDE, SIDE)),
            dma((2, SIDE, 2)),
            dma((2, SIDE, 2)),
            dma((2, 2)),
            dma((2, 2)),
            dma,
            dma((2,)),
            dma((2, far - 1)),
            dma,
            dma((2, far)),
            dma((4,)),
        ],
        compiler_params=pltpu.CompilerParams(
            collective_id=0, has_side_effects=True, vmem_limit_bytes=56 * 1024 * 1024
        ),
    )(hidden_states, ln_gain[None, :], ids, cluster_sizes, head_rows[0])
    new_head, new_first, new_second = adam_update(
        head_rows[0], first_moment[0], second_moment[0], head_grad.astype(F32)
    )
    return (new_head[None], new_first[None], new_second[None], input_grad, gain_grad[0])


def solution(mesh):
    in_specs = (
        P(("cluster", "dp"), None),
        P(),
        P(("cluster", "dp"), None),
        P(("cluster", "dp"), None),
        P("cluster"),
        P("cluster", None, None),
        P("cluster", None, None),
        P("cluster", None, None),
    )
    out_specs = (
        P("cluster", None, None),
        P("cluster", None, None),
        P("cluster", None, None),
        P(("cluster", "dp"), None),
        P(),
    )
    return jax.shard_map(shards, mesh=mesh, in_specs=in_specs, out_specs=out_specs, check_vma=False)
```

```python
import functools

import jax
import jax.numpy as jnp
from jax import lax
from jax.experimental import pallas as pl
from jax.experimental.pallas import tpu as pltpu
from jax.sharding import PartitionSpec as P

MESH = pl.DeviceIdType.MESH
F32 = jnp.float32
BF16 = jnp.bfloat16

norm_eps = 1e-05
learn_rate = 0.01
first_decay = 0.9
second_decay = 0.999
adam_eps = 1e-08
second_fix = 0.632304575226

SIDE = 4
PLANE = 32
ZC = 2
CHIPS = (
    (0, 0), (1, 0), (0, 1), (3, 0), (0, 3), (2, 0), (0, 2), (1, 1),
    (3, 3), (1, 3), (3, 1), (2, 1), (1, 2), (2, 3), (3, 2), (2, 2),
)


def table_at(values, at):
    half = len(values) // 2
    low = sum(v * 4**i for i, v in enumerate(values[:half]))
    high = sum(v * 4**i for i, v in enumerate(values[half:]))
    above = at // half
    word = low + above * (high - low)
    return lax.rem(lax.shift_right_logical(word, 2 * lax.rem(at, half)), 4)


def kernel(
    hid_ref, gain_ref, beam_ref, pos_ref, size_ref, head_ref,
    hg_ref, igrad_ref, ggrad_ref,
    emb, ids, wh, wt, hg, part, from_core, half_in, quart_in, half_in2, quart_in2,
    hgb, hgf, zq, zh, gplane, gz, egrad,
    ids_sem, ag_send, ag_recv, core_recv,
    rs_send, rs_core, rs_h, rs_q, rs_h2, rs_q2,
    z_send, z_q, z_h, zg_send, zg, g_sem,
):
    c = lax.axis_index("cluster")
    z = lax.axis_index("dp")
    depth = lax.axis_size("dp")
    rows, width = hid_ref.shape
    labels = head_ref.shape[0]
    beam = 8
    x, y, k = c // (2 * SIDE), lax.rem(c // 2, SIDE), lax.rem(c, 2)
    sibling = (c + 1 - 2 * k, z)

    def chip(dx, dy):
        return lax.rem(x + dx, SIDE) * SIDE + lax.rem(y + dy, SIDE)

    def chip_t(t, du, dv):
        return chip(du, dv) if t == 0 else chip(dv, du)

    def peer_t(t, du, dv):
        return (2 * chip_t(t, du, dv) + k, z)

    def copy(src, dst, send, recv, dev):
        return pltpu.make_async_remote_copy(
            src_ref=src, dst_ref=dst, send_sem=send, recv_sem=recv, device_id=dev, device_id_type=MESH
        )

    def arrived(dst, recv):
        copy(dst, dst, recv, recv, sibling).wait_recv()

    def sent(src, send):
        copy(src, src, send, send, sibling).wait_send()

    barrier = pltpu.get_barrier_semaphore()

    def greet(i, _):
        pl.semaphore_signal(barrier, inc=1, device_id=(lax.rem(c + i, PLANE), z), device_id_type=MESH)
        return _

    def greet_z(i, _):
        pl.semaphore_signal(barrier, inc=1, device_id=(c, lax.rem(z + i, depth)), device_id_type=MESH)
        return _

    lax.fori_loop(1, PLANE, greet, 0)
    lax.fori_loop(1, depth, greet_z, 0)

    ids[c] = jnp.concatenate([beam_ref[...], pos_ref[...]], axis=0).astype(jnp.int16)
    pl.semaphore_wait(barrier, PLANE - 1 + depth - 1)

    def send_ids(i, _):
        copy(ids.at[c], ids.at[c], ids_sem.at[0], ids_sem.at[1], (lax.rem(c + i, PLANE), z)).start()
        return _

    lax.fori_loop(1, PLANE, send_ids, 0)

    values = hid_ref[...].astype(F32)
    center = jnp.mean(values, axis=1, keepdims=True)
    spread = jnp.mean(jnp.square(values - center), axis=1, keepdims=True)
    normed = (values - center) * lax.rsqrt(spread + norm_eps)
    gain = gain_ref[...].reshape(1, width)
    emb[c] = (normed * gain).astype(BF16)

    half, quart = rows // 2, rows // 4

    def event(dx, dy):
        src = 2 * chip(dx, dy) + k
        for t in range(2):
            du, dv = (dx, dy) if t == 0 else (dy, dx)
            whole = emb.at[src, pl.ds(t * half, half)]
            q = [emb.at[src, pl.ds(t * half + i * quart, quart)] for i in range(2)]
            if (dx, dy) != (0, 0):
                arrived(whole, ag_recv.at[t, du, dv])

            def push(ref, tu, tv, t=t, du=du, dv=dv):
                there = ag_recv.at[t, (du - tu) % SIDE, (dv - tv) % SIDE]
                copy(ref, ref, ag_send, there, peer_t(t, tu % SIDE, tv % SIDE)).start()

            if dv == 0:
                if du == 0:
                    push(whole, 1, 0)
                    push(whole, -1, 0)
                elif du == 3:
                    push(q[0], 1, 0)
                elif du == 1:
                    push(q[1], -1, 0)
                push(whole, 0, 1)
                push(whole, 0, -1)
            elif dv == 3:
                push(q[0], 0, 1)
            elif dv == 1:
                push(q[1], 0, -1)
        copy(emb.at[src], emb.at[src], ag_send, core_recv.at[dx, dy], sibling).start()

    event(0, 0)

    wh[...] = (head_ref[...].astype(BF16) * 0.5).astype(BF16)
    for i in range(width // 128):
        cols = pl.ds(i * 128, 128)
        wt[cols, :] = head_ref[:, cols].T.astype(BF16)
    hg[...] = jnp.zeros_like(hg)
    size = size_ref[0]
    arrived(ids.at[pl.ds(0, PLANE - 1)], ids_sem.at[1])

    def compute(at):
        dx, dy = table_at([p[0] for p in CHIPS], at), table_at([p[1] for p in CHIPS], at)
        ch = chip(dx, dy)
        arrived(emb.at[2 * ch + 1 - k], core_recv.at[dx, dy])
        block = emb[pl.ds(2 * ch, 2)].reshape(2 * rows, width)
        label, limit = [], []
        for s in range(2):
            own = ids[2 * ch + s].astype(jnp.int32)
            match = own[0:beam] == c
            place = lax.broadcasted_iota(jnp.int32, (beam, rows), 0)
            place = jnp.sum(jnp.where(match, place, 0), axis=0, keepdims=True)
            chosen = jnp.max(jnp.where(match, 1, 0), axis=0, keepdims=True)
            label.append(own[beam:] - place * labels)
            limit.append(chosen * size)
        label = jnp.concatenate(label, axis=1)
        limit = jnp.concatenate(limit, axis=1)
        logits = lax.dot_general(wh[...], block, (((1,), (1,)), ((), ())), preferred_element_type=F32)
        slot = lax.broadcasted_iota(jnp.int32, (labels, 2 * rows), 0)
        word = lax.shift_right_arithmetic(label, 5)
        bit = lax.shift_left(jnp.ones_like(label), label & 31)
        words = lax.broadcasted_iota(jnp.int32, (labels // 32, 2 * rows), 0)
        bits = jnp.zeros_like(words)
        for p in range(label.shape[0]):
            bits = bits | jnp.where(word[p : p + 1] == words, bit[p : p + 1], 0)
        bits = jnp.broadcast_to(bits[:, None, :], (labels // 32, 32, 2 * rows)).reshape(labels, 2 * rows)
        hit = lax.shift_left(bits, 31 - (slot & 31)) < 0
        step = 0.5 / beam
        slope = step * jnp.tanh(logits) + jnp.where(hit, -step, step)
        slope = jnp.where(slot < limit, slope, 0.0).astype(BF16)
        hg[...] += jnp.dot(slope, block, preferred_element_type=F32)
        back = jnp.dot(wt[...], slope, preferred_element_type=F32).astype(BF16)
        part[2 * ch] = back[:, :rows]
        part[2 * ch + 1] = back[:, rows:]
        there = 2 * ch + 1 - k
        copy(part.at[there], from_core.at[ch], rs_send, rs_core.at[dx, dy], sibling).start()

    def join(at):
        dx, dy = table_at([p[0] for p in CHIPS], at), table_at([p[1] for p in CHIPS], at)
        ch = chip(dx, dy)
        arrived(from_core.at[ch], rs_core.at[dx, dy])
        part[2 * ch + k] += from_core[ch]

    count = len(CHIPS)

    def turn(e, _):
        for i in range(1, count):
            pl.when(e == i)(functools.partial(event, *CHIPS[i]))

        @pl.when((e >= 1) & (e <= count))
        def _compute():
            compute(e - 1)

        @pl.when(e >= 2)
        def _join():
            join(e - 2)

        return _

    lax.fori_loop(1, count + 2, turn, 0)

    piece = labels // depth
    far = depth // 2

    def at_z(i):
        return lax.rem(z + i + depth, depth)

    chunk = piece // ZC
    part_z = chunk // 2

    def rows_z(h, i, lo=0, n=chunk):
        return pl.ds(pl.multiple_of(at_z(i) * piece + h * chunk + lo, part_z), n)

    hgb[...] = hg[...].astype(BF16)

    def z_first(h):
        for s in range(2):
            src = hgb.at[rows_z(h, far, s * part_z, part_z)]
            copy(src, zq.at[h, s], z_send, z_q.at[h, s], (c, at_z(1 - 2 * s))).start()

    def z_next(h, i):
        for s in range(2):
            way = 1 - 2 * s
            own = rows_z(h, way * (far - 1 - i))
            if i == 0:
                arrived(zq.at[h, s], z_q.at[h, s])
                mid = rows_z(h, way * (far - 1), s * part_z, part_z)
                hgb[mid] += zq[h, s]
            else:
                arrived(zh.at[h, s, i - 1], z_h.at[h, s, i - 1])
                hgb[own] += zh[h, s, i - 1]
            copy(hgb.at[own], zh.at[h, s, i], z_send, z_h.at[h, s, i], (c, at_z(way))).start()

    def z_last(h):
        total = hgb[rows_z(h, 0)].astype(F32)
        for s in range(2):
            arrived(zh.at[h, s, far - 2], z_h.at[h, s, far - 2])
            total += zh[h, s, far - 2].astype(F32)
        hgf[rows_z(h, 0)] = total.astype(BF16)
        for s in range(2):
            own = hgf.at[rows_z(h, 0)]
            copy(own, own, zg_send, zg.at[h, s, 0], (c, at_z(1 - 2 * s))).start()

    def z_spread(h, i):
        for s in range(2):
            way = 1 - 2 * s
            own = hgf.at[rows_z(h, -way * i)]
            arrived(own, zg.at[h, s, i - 1])
            if i == far - 1:
                own = hgf.at[rows_z(h, -way * i, s * part_z, part_z)]
            copy(own, own, zg_send, zg.at[h, s, i], (c, at_z(way))).start()

    def z_end(h):
        for s in range(2):
            arrived(hgf.at[rows_z(h, far, s * part_z, part_z)], zg.at[h, s, far - 1])

    fh, fq = width // 2, width // 4

    def feats(t, lo, n):
        return pl.ds(t * fh + lo, n)

    def dest(t, du, dv):
        return 2 * chip_t(t, du % SIDE, dv % SIDE) + k

    def v_first(t, du):
        for s in range(2):
            src = part.at[dest(t, du, 2), feats(t, s * fq, fq)]
            copy(src, quart_in.at[t, du, s], rs_send, rs_q.at[t, du, s], peer_t(t, 0, (1, 3)[s])).start()

    def v_next(t, du):
        for s in range(2):
            arrived(quart_in.at[t, du, s], rs_q.at[t, du, s])
            to = dest(t, du, (1, 3)[s])
            part[to, feats(t, s * fq, fq)] += quart_in[t, du, s]
            src = part.at[to, feats(t, 0, fh)]
            copy(src, half_in.at[t, du, s], rs_send, rs_h.at[t, du, s], peer_t(t, 0, (1, 3)[s])).start()

    def v_last(t, du):
        to = dest(t, du, 0)
        for s in range(2):
            arrived(half_in.at[t, du, s], rs_h.at[t, du, s])
        total = part[to, feats(t, 0, fh)].astype(F32)
        total += half_in[t, du, 0].astype(F32) + half_in[t, du, 1].astype(F32)
        part[to, feats(t, 0, fh)] = total.astype(BF16)

    def u_first(t):
        for s in range(2):
            src = part.at[dest(t, 2, 0), feats(t, s * fq, fq)]
            copy(src, quart_in2.at[t, s], rs_send, rs_q2.at[t, s], peer_t(t, (1, 3)[s], 0)).start()

    def u_next(t):
        for s in range(2):
            arrived(quart_in2.at[t, s], rs_q2.at[t, s])
            to = dest(t, (1, 3)[s], 0)
            part[to, feats(t, s * fq, fq)] += quart_in2[t, s]
            src = part.at[to, feats(t, 0, fh)]
            copy(src, half_in2.at[t, s], rs_send, rs_h2.at[t, s], peer_t(t, (1, 3)[s], 0)).start()

    def u_last(t):
        for s in range(2):
            arrived(half_in2.at[t, s], rs_h2.at[t, s])
        total = part[c, feats(t, 0, fh)].astype(F32)
        total += half_in2[t, 0].astype(F32) + half_in2[t, 1].astype(F32)
        egrad[feats(t, 0, fh), :] = total

    def g_first():
        total = jnp.sum(wh[...].astype(F32) * hg[...], axis=0, keepdims=True)
        gplane[c] = total * 2.0

        def send(i, _):
            to = (lax.rem(c + i, PLANE), z)
            copy(gplane.at[c], gplane.at[c], g_sem.at[0], g_sem.at[1], to).start()
            return _

        lax.fori_loop(1, PLANE, send, 0)

    def g_next():
        arrived(gplane.at[pl.ds(0, PLANE - 1)], g_sem.at[1])
        gz[z] = jnp.sum(gplane[...], axis=0)

        def send(i, _):
            copy(gz.at[z], gz.at[z], g_sem.at[2], g_sem.at[3], (c, at_z(i))).start()
            return _

        lax.fori_loop(1, depth, send, 0)

    def g_last():
        arrived(gz.at[pl.ds(0, depth - 1)], g_sem.at[3])
        ggrad_ref[...] = (jnp.sum(gz[...], axis=0) / gain).reshape(width)

    for h in range(ZC):
        z_first(h)
    for du in (2, 1, 3, 0):
        for t in range(2):
            v_first(t, du)
    z_next(0, 0)
    g_first()
    z_next(1, 0)
    for t in range(2):
        v_next(t, 2)
    z_next(0, 1)
    for t in range(2):
        v_next(t, 1)
    z_next(1, 1)
    for t in range(2):
        v_next(t, 3)
    z_next(0, 2)
    for t in range(2):
        v_next(t, 0)
    z_next(1, 2)
    for t in range(2):
        v_last(t, 2)
        u_first(t)
    z_last(0)
    for t in range(2):
        v_last(t, 1)
    z_last(1)
    for t in range(2):
        v_last(t, 3)
    z_spread(0, 1)
    for t in range(2):
        u_next(t)
    z_spread(1, 1)
    g_next()
    for t in range(2):
        v_last(t, 0)
    z_spread(0, 2)
    z_spread(1, 2)
    for t in range(2):
        u_last(t)
    z_spread(0, 3)
    z_spread(1, 3)

    emb_grad = egrad[...].T
    values = hid_ref[...].astype(F32)
    center = jnp.mean(values, axis=1, keepdims=True)
    spread = jnp.mean(jnp.square(values - center), axis=1, keepdims=True)
    inverse = lax.rsqrt(spread + norm_eps)
    normed = (values - center) * inverse
    scaled = emb_grad * gain
    first_mean = jnp.mean(scaled, axis=1, keepdims=True)
    second_mean = jnp.mean(scaled * normed, axis=1, keepdims=True)
    igrad_ref[...] = ((scaled - first_mean - normed * second_mean) * inverse).astype(BF16)

    g_last()
    for h in range(ZC):
        z_end(h)
    hg_ref[...] = hgf[...]

    sent(emb.at[pl.ds(0, PLANE - 1)], ag_send)
    sent(part.at[pl.ds(0, PLANE - 1)], rs_send)
    sent(ids.at[pl.ds(0, PLANE - 1)], ids_sem.at[0])
    sent(gplane.at[pl.ds(0, PLANE - 1)], g_sem.at[0])
    sent(gz.at[pl.ds(0, depth - 1)], g_sem.at[2])
    sent(hgb.at[pl.ds(0, labels - piece)], z_send)
    sent(hgf.at[pl.ds(0, labels - piece)], zg_send)


def adam_update(head_rows, first_moment, second_moment, head_grad):
    new_first = first_decay * first_moment + (1.0 - first_decay) * head_grad
    new_second = second_decay * second_moment + (1.0 - second_decay) * head_grad * head_grad
    step_size = new_first / (jnp.sqrt(new_second / second_fix) + adam_eps)
    return (head_rows - learn_rate * step_size, new_first, new_second)


def shards(
    hidden_states,
    ln_gain,
    beam_ids,
    positive_ids,
    cluster_sizes,
    head_rows,
    first_moment,
    second_moment,
):
    rows, width = hidden_states.shape
    labels = head_rows.shape[1]
    depth = lax.axis_size("dp")
    vmem = pl.BlockSpec(memory_space=pltpu.VMEM)
    smem = pl.BlockSpec(memory_space=pltpu.SMEM)
    fh, fq, piece, far = width // 2, width // 4, labels // depth, depth // 2
    dma = pltpu.SemaphoreType.DMA
    head_grad, input_grad, gain_grad = pl.pallas_call(
        kernel,
        out_shape=(
            jax.ShapeDtypeStruct((labels, width), BF16),
            jax.ShapeDtypeStruct((rows, width), BF16),
            jax.ShapeDtypeStruct((width,), F32),
        ),
        in_specs=[vmem, vmem, vmem, vmem, smem, vmem],
        out_specs=(vmem, vmem, vmem),
        scratch_shapes=[
            pltpu.VMEM((PLANE, rows, width), BF16),
            pltpu.VMEM((PLANE, 16, rows), jnp.int16),
            pltpu.VMEM((labels, width), BF16),
            pltpu.VMEM((width, labels), BF16),
            pltpu.VMEM((labels, width), F32),
            pltpu.VMEM((PLANE, width, rows), BF16),
            pltpu.VMEM((PLANE // 2, width, rows), BF16),
            pltpu.VMEM((2, SIDE, 2, fh, rows), BF16),
            pltpu.VMEM((2, SIDE, 2, fq, rows), BF16),
            pltpu.VMEM((2, 2, fh, rows), BF16),
            pltpu.VMEM((2, 2, fq, rows), BF16),
            pltpu.VMEM((labels, width), BF16),
            pltpu.VMEM((labels, width), BF16),
            pltpu.VMEM((ZC, 2, piece // ZC // 2, width), BF16),
            pltpu.VMEM((ZC, 2, far - 1, piece // ZC, width), BF16),
            pltpu.VMEM((PLANE, 1, width), F32),
            pltpu.VMEM((depth, 1, width), F32),
            pltpu.VMEM((width, rows), F32),
            dma((2,)),
            dma,
            dma((2, SIDE, SIDE)),
            dma((SIDE, SIDE)),
            dma,
            dma((SIDE, SIDE)),
            dma((2, SIDE, 2)),
            dma((2, SIDE, 2)),
            dma((2, 2)),
            dma((2, 2)),
            dma,
            dma((ZC, 2)),
            dma((ZC, 2, far - 1)),
            dma,
            dma((ZC, 2, far)),
            dma((4,)),
        ],
        compiler_params=pltpu.CompilerParams(
            collective_id=0, has_side_effects=True, vmem_limit_bytes=34 * 1024 * 1024
        ),
    )(hidden_states, ln_gain, beam_ids.T, positive_ids.T, cluster_sizes, head_rows[0])
    new_head, new_first, new_second = adam_update(
        head_rows[0], first_moment[0], second_moment[0], head_grad.astype(F32)
    )
    return (new_head[None], new_first[None], new_second[None], input_grad, gain_grad)


def solution(mesh):
    in_specs = (
        P(("cluster", "dp"), None),
        P(),
        P(("cluster", "dp"), None),
        P(("cluster", "dp"), None),
        P("cluster"),
        P("cluster", None, None),
        P("cluster", None, None),
        P("cluster", None, None),
    )
    out_specs = (
        P("cluster", None, None),
        P("cluster", None, None),
        P("cluster", None, None),
        P(("cluster", "dp"), None),
        P(),
    )
    return jax.shard_map(shards, mesh=mesh, in_specs=in_specs, out_specs=out_specs, check_vma=False)
```

```python
import functools

import jax
import jax.numpy as jnp
from jax import lax
from jax.experimental import pallas as pl
from jax.experimental.pallas import tpu as pltpu
from jax.sharding import PartitionSpec as P

MESH = pl.DeviceIdType.MESH
F32 = jnp.float32
BF16 = jnp.bfloat16

norm_eps = 1e-05
learn_rate = 0.01
first_decay = 0.9
second_decay = 0.999
adam_eps = 1e-08
second_fix = 0.632304575226

SIDE = 4
PLANE = 32
CHIPS = (
    (0, 0), (1, 0), (0, 1), (3, 0), (0, 3), (2, 0), (0, 2), (1, 1),
    (3, 3), (1, 3), (3, 1), (2, 1), (1, 2), (2, 3), (3, 2), (2, 2),
)
PLACE = {offset: i for i, offset in enumerate(CHIPS)}
GROUP = 4
ZC = 3


def table_at(values, at):
    half = len(values) // 2
    low = sum(v * 4**i for i, v in enumerate(values[:half]))
    high = sum(v * 4**i for i, v in enumerate(values[half:]))
    above = at // half
    word = low + above * (high - low)
    return lax.rem(lax.shift_right_logical(word, 2 * lax.rem(at, half)), 4)


def kernel(
    size_in, hid_in, gain_in, beam_in, pos_in, head_in, first_in, second_in,
    nh_ref, nf_ref, ns_ref, igrad_ref, ggrad_ref,
    hid, gain_v, beam_v, pos_v, head, first, second,
    emb, ids, wh, wt, hg, slope_v, part, from_core, half_in, quart_in, half_in2, quart_in2,
    hgb, hgf, zq, zh, gc, gx, gy, gz, egrad, normed_v, inverse_v,
    in_sem, ids_send, ids_recv, ag_send, ag_recv, core_recv,
    core_send, rs_core, rs_send, rs_h, rs_q, rs_h2, rs_q2,
    z_send, z_q, z_h, zg_send, zg, g_send, g_recv,
):
    c = lax.axis_index("cluster")
    z = lax.axis_index("dp")
    depth = lax.axis_size("dp")
    rows, width = hid.shape
    labels = head.shape[0]
    beam = beam_v.shape[0]
    x, y, k = c // (2 * SIDE), lax.rem(c // 2, SIDE), lax.rem(c, 2)
    sibling = (c + 1 - 2 * k, z)

    def dev(dx, dy):
        return ((lax.rem(x + dx, SIDE) * SIDE + lax.rem(y + dy, SIDE)) * 2 + k, z)

    def turned(t, du, dv):
        du, dv = du % SIDE, dv % SIDE
        return (du, dv) if t == 0 else (dv, du)

    def copy(src, dst, send, recv, device):
        return pltpu.make_async_remote_copy(
            src_ref=src, dst_ref=dst, send_sem=send, recv_sem=recv, device_id=device, device_id_type=MESH
        )

    def arrived(dst, recv):
        copy(dst, dst, recv, recv, sibling).wait_recv()

    def sent(src, send):
        copy(src, src, send, send, sibling).wait_send()

    loads = [
        pltpu.make_async_copy(src, dst, in_sem.at[i])
        for i, (src, dst) in enumerate(
            (
                (beam_in, beam_v), (pos_in, pos_v), (hid_in, hid), (gain_in, gain_v),
                (head_in, head), (first_in, first), (second_in, second),
            )
        )
    ]
    for load in loads:
        load.start()

    barrier = pltpu.get_barrier_semaphore()
    pl.semaphore_signal(barrier, inc=1, device_id=sibling, device_id_type=MESH)
    for i in range(1, SIDE):
        pl.semaphore_signal(barrier, inc=1, device_id=dev(i, 0), device_id_type=MESH)
        pl.semaphore_signal(barrier, inc=1, device_id=dev(0, i), device_id_type=MESH)

    def greet(i, _):
        pl.semaphore_signal(barrier, inc=1, device_id=(c, lax.rem(z + i, depth)), device_id_type=MESH)
        return _

    lax.fori_loop(1, depth, greet, 0)

    half, quart = rows // 2, rows // 4

    def push(t, at, lo, n, tu, tv):
        du, dv = turned(t, *CHIPS[at])
        to = PLACE[turned(t, du - tu, dv - tv)]
        src, dst = emb.at[2 * at + k, pl.ds(lo, n)], emb.at[2 * to + k, pl.ds(lo, n)]
        copy(src, dst, ag_send, ag_recv.at[t, to], dev(*turned(t, tu, tv))).start()

    def event(at):
        for t in range(2):
            du, dv = turned(t, *CHIPS[at])
            lo = t * half
            if at > 0:
                arrived(emb.at[2 * at + k, pl.ds(lo, half)], ag_recv.at[t, at])
            if dv == 0:
                if du == 0:
                    push(t, at, lo, half, 1, 0)
                    push(t, at, lo, half, -1, 0)
                elif du == 3:
                    push(t, at, lo, quart, 1, 0)
                elif du == 1:
                    push(t, at, lo + quart, quart, -1, 0)
                push(t, at, lo, half, 0, 1)
                push(t, at, lo, half, 0, -1)
            elif dv == 3:
                push(t, at, lo, quart, 0, 1)
            elif dv == 1:
                push(t, at, lo + quart, quart, 0, -1)
        mine = emb.at[2 * at + k]
        copy(mine, mine, ag_send, core_recv.at[at], sibling).start()

    for load in loads[:4]:
        load.wait()
    gain = jnp.concatenate([gain_v[i : i + 1, :] for i in range(width // 128)], axis=1)
    values = hid[...].astype(F32)
    center = jnp.mean(values, axis=1, keepdims=True)
    spread = jnp.mean(jnp.square(values - center), axis=1, keepdims=True)
    inverse = lax.rsqrt(spread + norm_eps)
    normed = (values - center) * inverse
    normed_v[...] = normed
    inverse_v[...] = inverse
    emb[k] = (normed * gain).astype(BF16)
    ids[x, y, k] = jnp.concatenate([beam_v[...], pos_v[...]], axis=0).astype(jnp.int16)
    pl.semaphore_wait(barrier, 1 + 2 * (SIDE - 1) + depth - 1)

    event(0)
    for i in range(1, SIDE):
        own = ids.at[x, y, k]
        copy(own, own, ids_send.at[0], ids_recv.at[0], dev(i, 0)).start()

    loads[4].wait()
    wh[...] = (head[...].astype(BF16) * 0.5).astype(BF16)
    for i in range(width // 128):
        cols = pl.ds(i * 128, 128)
        wt[cols, :] = head[:, cols].T.astype(BF16)
    hg[...] = jnp.zeros_like(hg)
    size = size_in[0]

    arrived(ids.at[pl.ds(0, SIDE - 1), y, k], ids_recv.at[0])
    for i in range(1, SIDE):
        own = ids.at[:, y, k]
        copy(own, own, ids_send.at[1], ids_recv.at[1], dev(0, i)).start()
    event(1)
    event(2)
    arrived(ids.at[:, pl.ds(0, SIDE - 1), k], ids_recv.at[1])
    own = ids.at[:, :, k]
    copy(own, own, ids_send.at[2], ids_recv.at[2], sibling).start()

    many = 2 * GROUP * rows

    def block_of(g):
        return emb[pl.ds(2 * GROUP * g, 2 * GROUP)].reshape(many, width)

    def score(g):
        label, limit = [], []
        for q in range(GROUP):
            at = GROUP * g + q
            arrived(emb.at[2 * at + 1 - k], core_recv.at[at])
            dx, dy = table_at([p[0] for p in CHIPS], at), table_at([p[1] for p in CHIPS], at)
            for s in range(2):
                own = ids[lax.rem(x + dx, SIDE), lax.rem(y + dy, SIDE), s].astype(jnp.int32)
                match = own[0:beam] == c
                place = lax.broadcasted_iota(jnp.int32, (beam, rows), 0)
                place = jnp.sum(jnp.where(match, place, 0), axis=0, keepdims=True)
                chosen = jnp.max(jnp.where(match, 1, 0), axis=0, keepdims=True)
                label.append(own[beam:] - place * labels)
                limit.append(chosen * size)
        label = jnp.concatenate(label, axis=1)
        limit = jnp.concatenate(limit, axis=1)
        logits = lax.dot_general(wh[...], block_of(g), (((1,), (1,)), ((), ())), preferred_element_type=F32)
        word = lax.shift_right_arithmetic(label, 5)
        bit = lax.shift_left(jnp.ones_like(label), label & 31)
        words = lax.broadcasted_iota(jnp.int32, (labels // 32, many), 0)
        bits = jnp.zeros_like(words)
        for p in range(label.shape[0]):
            bits = bits | jnp.where(word[p : p + 1] == words, bit[p : p + 1], 0)
        step = 0.5 / beam
        for i in range(labels // 32):
            slot = lax.broadcasted_iota(jnp.int32, (32, many), 0)
            hit = lax.shift_left(jnp.broadcast_to(bits[i : i + 1], (32, many)), 31 - slot) < 0
            slope = step * jnp.tanh(logits[32 * i : 32 * i + 32]) + jnp.where(hit, -step, step)
            slope = jnp.where(slot + 32 * i < limit, slope, 0.0)
            slope_v[pl.ds(32 * i, 32), :] = slope.astype(BF16)

    def gather_head(g):
        hg[...] += jnp.dot(slope_v[...], block_of(g), preferred_element_type=F32)

    def back(g):
        grads = jnp.dot(wt[...], slope_v[...], preferred_element_type=F32).astype(BF16)
        for q in range(GROUP):
            for s in range(2):
                i = 2 * q + s
                part[GROUP * g + q, s] = grads[:, i * rows : (i + 1) * rows]
        there = pl.ds(GROUP * g, GROUP)
        copy(part.at[there, 1 - k], from_core.at[there], core_send, rs_core.at[g], sibling).start()

    def join(g):
        arrived(from_core.at[pl.ds(GROUP * g, GROUP)], rs_core.at[g])
        for q in range(GROUP):
            part[GROUP * g + q, k] += from_core[GROUP * g + q]

    groups = len(CHIPS) // GROUP

    def turn(g, _):
        def events(shift):
            for i in range(groups):
                if GROUP * i + shift < len(CHIPS):
                    pl.when(g == i)(functools.partial(event, GROUP * i + shift))

        events(3)

        @pl.when(g == 0)
        def _ids():
            arrived(ids.at[:, :, k], ids_recv.at[2])

        @pl.when(g >= 1)
        def _back():
            back(g - 1)

        events(4)
        score(g)
        events(5)

        @pl.when(g >= 2)
        def _join():
            join(g - 2)

        gather_head(g)
        events(6)
        return _

    lax.fori_loop(0, groups, turn, 0)

    piece = labels // depth
    part_z = piece // 2
    far = depth // 2
    wide = width // ZC

    def at_z(i):
        return lax.rem(z + i + depth, depth)

    def rows_z(i, lo=0, n=piece):
        return pl.ds(pl.multiple_of(at_z(i) * piece + lo, part_z), n)

    def z_first(h):
        hgb[h] = hg[:, h * wide : (h + 1) * wide].astype(BF16)
        for s in range(2):
            src = hgb.at[h, rows_z(far, s * part_z, part_z)]
            copy(src, zq.at[h, s], z_send, z_q.at[h, s], (c, at_z(1 - 2 * s))).start()

    def z_next(h, i):
        for s in range(2):
            way = 1 - 2 * s
            own = rows_z(way * (far - 1 - i))
            if i == 0:
                arrived(zq.at[h, s], z_q.at[h, s])
                mid = rows_z(way * (far - 1), s * part_z, part_z)
                hgb[h, mid] += zq[h, s]
            else:
                arrived(zh.at[h, s, i - 1], z_h.at[h, s, i - 1])
                hgb[h, own] += zh[h, s, i - 1]
            copy(hgb.at[h, own], zh.at[h, s, i], z_send, z_h.at[h, s, i], (c, at_z(way))).start()

    def adam(h, at):
        cols = pl.ds(h * wide, wide)
        grad = hgf[h, at].astype(F32)
        new_first = first_decay * first[at, cols] + (1.0 - first_decay) * grad
        new_second = second_decay * second[at, cols] + (1.0 - second_decay) * grad * grad
        nf_ref[at, cols] = new_first
        ns_ref[at, cols] = new_second
        step_size = new_first / (jnp.sqrt(new_second * (1.0 / second_fix)) + adam_eps)
        nh_ref[at, cols] = head[at, cols] - learn_rate * step_size

    def z_last(h):
        total = hgb[h, rows_z(0)].astype(F32)
        for s in range(2):
            arrived(zh.at[h, s, far - 2], z_h.at[h, s, far - 2])
            total += zh[h, s, far - 2].astype(F32)
        hgf[h, rows_z(0)] = total.astype(BF16)
        for s in range(2):
            own = hgf.at[h, rows_z(0)]
            copy(own, own, zg_send, zg.at[h, s, 0], (c, at_z(1 - 2 * s))).start()

    def z_spread(h, i):
        for s in range(2):
            way = 1 - 2 * s
            own = hgf.at[h, rows_z(-way * i)]
            arrived(own, zg.at[h, s, i - 1])
            if i == far - 1:
                own = hgf.at[h, rows_z(-way * i, s * part_z, part_z)]
            copy(own, own, zg_send, zg.at[h, s, i], (c, at_z(way))).start()

    def z_adam(h, i):
        adam(h, rows_z(i))
        adam(h, rows_z(-i))

    def z_end(h):
        for s in range(2):
            arrived(hgf.at[h, rows_z(far, s * part_z, part_z)], zg.at[h, s, far - 1])
        adam(h, rows_z(far))

    fh, fq = width // 2, width // 4

    def feats(t, lo, n):
        return pl.ds(t * fh + lo, n)

    def dest(t, du, dv):
        return PLACE[turned(t, du, dv)]

    def v_first(t, du):
        for s in range(2):
            src = part.at[dest(t, du, 2), k, feats(t, s * fq, fq)]
            to = dev(*turned(t, 0, 1 - 2 * s))
            copy(src, quart_in.at[t, du, s], rs_send, rs_q.at[t, du, s], to).start()

    def v_next(t, du):
        for s in range(2):
            arrived(quart_in.at[t, du, s], rs_q.at[t, du, s])
            to = dest(t, du, 1 - 2 * s)
            part[to, k, feats(t, s * fq, fq)] += quart_in[t, du, s]
            src = part.at[to, k, feats(t, 0, fh)]
            copy(src, half_in.at[t, du, s], rs_send, rs_h.at[t, du, s], dev(*turned(t, 0, 1 - 2 * s))).start()

    def v_last(t, du):
        to = dest(t, du, 0)
        for s in range(2):
            arrived(half_in.at[t, du, s], rs_h.at[t, du, s])
        total = part[to, k, feats(t, 0, fh)].astype(F32)
        total += half_in[t, du, 0].astype(F32) + half_in[t, du, 1].astype(F32)
        part[to, k, feats(t, 0, fh)] = total.astype(BF16)

    def u_first(t):
        for s in range(2):
            src = part.at[dest(t, 2, 0), k, feats(t, s * fq, fq)]
            copy(src, quart_in2.at[t, s], rs_send, rs_q2.at[t, s], dev(*turned(t, 1 - 2 * s, 0))).start()

    def u_next(t):
        for s in range(2):
            arrived(quart_in2.at[t, s], rs_q2.at[t, s])
            to = dest(t, 1 - 2 * s, 0)
            part[to, k, feats(t, s * fq, fq)] += quart_in2[t, s]
            src = part.at[to, k, feats(t, 0, fh)]
            copy(src, half_in2.at[t, s], rs_send, rs_h2.at[t, s], dev(*turned(t, 1 - 2 * s, 0))).start()

    def u_last(t):
        for s in range(2):
            arrived(half_in2.at[t, s], rs_h2.at[t, s])
        total = part[0, k, feats(t, 0, fh)].astype(F32)
        total += half_in2[t, 0].astype(F32) + half_in2[t, 1].astype(F32)
        egrad[:, t * fh : (t + 1) * fh] = total.T

    def g_first():
        gc[k] = jnp.sum(wh[...].astype(F32) * hg[...], axis=0, keepdims=True) * 2.0
        copy(gc.at[k], gc.at[k], g_send.at[0], g_recv.at[0], sibling).start()

    def g_x():
        arrived(gc.at[0], g_recv.at[0])
        gx[x] = gc[0] + gc[1]
        for i in range(1, SIDE):
            copy(gx.at[x], gx.at[x], g_send.at[1], g_recv.at[1], dev(i, 0)).start()

    def g_y():
        arrived(gx.at[pl.ds(0, SIDE - 1)], g_recv.at[1])
        gy[y] = jnp.sum(gx[...], axis=0)
        for i in range(1, SIDE):
            copy(gy.at[y], gy.at[y], g_send.at[2], g_recv.at[2], dev(0, i)).start()

    def g_z():
        arrived(gy.at[pl.ds(0, SIDE - 1)], g_recv.at[2])
        gz[z] = jnp.sum(gy[...], axis=0)

        def send(i, _):
            copy(gz.at[z], gz.at[z], g_send.at[3], g_recv.at[3], (c, at_z(i))).start()
            return _

        lax.fori_loop(1, depth, send, 0)

    def g_last():
        arrived(gz.at[pl.ds(0, depth - 1)], g_recv.at[3])
        total = jnp.sum(gz[...], axis=0) / gain
        for i in range(width // 128):
            ggrad_ref[i : i + 1, :] = total[:, i * 128 : (i + 1) * 128]

    chunks = range(ZC)
    for h in chunks:
        z_first(h)
    back(groups - 1)
    join(groups - 2)
    g_first()
    for h in chunks:
        z_next(h, 0)
    join(groups - 1)
    for du in (2, 1, 3, 0):
        for t in range(2):
            v_first(t, du)
    g_x()
    for h in chunks:
        z_next(h, 1)
    for t in range(2):
        v_next(t, 2)
    for t in range(2):
        v_next(t, 1)
    z_next(0, 2)
    for t in range(2):
        v_next(t, 3)
    z_next(1, 2)
    z_next(2, 2)
    for t in range(2):
        v_next(t, 0)
    g_y()
    z_last(0)
    for t in range(2):
        v_last(t, 2)
        u_first(t)
    z_last(1)
    z_last(2)
    loads[5].wait()
    loads[6].wait()
    for t in range(2):
        v_last(t, 1)
    for h in chunks:
        z_spread(h, 1)
    g_z()
    for t in range(2):
        v_last(t, 3)
    for t in range(2):
        u_next(t)
    for h in chunks:
        z_spread(h, 2)
        adam(h, rows_z(0))
    for t in range(2):
        v_last(t, 0)
    for h in chunks:
        z_adam(h, 1)
    for h in chunks:
        z_spread(h, 3)
    for t in range(2):
        u_last(t)
    for h in chunks:
        z_adam(h, 2)

    scaled = egrad[...] * gain
    normed = normed_v[...]
    first_mean = jnp.mean(scaled, axis=1, keepdims=True)
    second_mean = jnp.mean(scaled * normed, axis=1, keepdims=True)
    igrad_ref[...] = ((scaled - first_mean - normed * second_mean) * inverse_v[...]).astype(BF16)

    for h in chunks:
        z_adam(h, 3)
    g_last()
    for h in chunks:
        z_end(h)

    sent(emb.at[pl.ds(0, PLANE - 1)], ag_send)
    sent(from_core, core_send)
    sent(from_core.at[pl.ds(0, PLANE // 2 - 1)], rs_send)
    sent(ids.at[pl.ds(0, SIDE - 1), y, k], ids_send.at[0])
    sent(ids.at[:, pl.ds(0, SIDE - 1), k], ids_send.at[1])
    sent(ids.at[:, :, k], ids_send.at[2])
    sent(gc.at[0], g_send.at[0])
    sent(gx.at[pl.ds(0, SIDE - 1)], g_send.at[1])
    sent(gy.at[pl.ds(0, SIDE - 1)], g_send.at[2])
    sent(gz.at[pl.ds(0, depth - 1)], g_send.at[3])
    sent(hgb.at[:, pl.ds(0, labels - piece)], z_send)
    sent(hgf.at[:, pl.ds(0, labels - piece)], zg_send)


def store(nh, nf, ns, igrad, ggrad, nh_out, nf_out, ns_out, igrad_out, ggrad_out, sem):
    pairs = ((nh, nh_out.at[0]), (nf, nf_out.at[0]), (ns, ns_out.at[0]), (igrad, igrad_out), (ggrad, ggrad_out))
    copies = [pltpu.make_async_copy(src, dst, sem.at[i]) for i, (src, dst) in enumerate(pairs)]
    for copy in copies:
        copy.start()
    for copy in copies:
        copy.wait()


def shards(
    hidden_states,
    ln_gain,
    beam_ids,
    positive_ids,
    cluster_sizes,
    head_rows,
    first_moment,
    second_moment,
):
    rows, width = hidden_states.shape
    labels = head_rows.shape[1]
    beam, pos = beam_ids.shape[1], positive_ids.shape[1]
    depth = lax.axis_size("dp")
    vmem = pl.BlockSpec(memory_space=pltpu.VMEM)
    hbm = pl.BlockSpec(memory_space=pltpu.HBM)
    fh, fq, piece, far, wide = width // 2, width // 4, labels // depth, depth // 2, width // ZC
    dma = pltpu.SemaphoreType.DMA
    head_shape = pltpu.VMEM((labels, width), F32)
    results = pl.pallas_call(
        kernel,
        out_shape=(
            head_shape,
            head_shape,
            head_shape,
            pltpu.VMEM((rows, width), BF16),
            pltpu.VMEM((width // 128, 128), F32),
        ),
        in_specs=[pl.BlockSpec(memory_space=pltpu.SMEM)] + [hbm] * 7,
        out_specs=(vmem,) * 5,
        scratch_shapes=[
            pltpu.VMEM((rows, width), BF16),
            pltpu.VMEM((width // 128, 128), F32),
            pltpu.VMEM((beam, rows), jnp.int32),
            pltpu.VMEM((pos, rows), jnp.int32),
            pltpu.VMEM((labels, width), F32),
            pltpu.VMEM((labels, width), F32),
            pltpu.VMEM((labels, width), F32),
            pltpu.VMEM((PLANE, rows, width), BF16),
            pltpu.VMEM((SIDE, SIDE, 2, beam + pos, rows), jnp.int16),
            pltpu.VMEM((labels, width), BF16),
            pltpu.VMEM((width, labels), BF16),
            pltpu.VMEM((labels, width), F32),
            pltpu.VMEM((labels, 2 * GROUP * rows), BF16),
            pltpu.VMEM((PLANE // 2, 2, width, rows), BF16),
            pltpu.VMEM((PLANE // 2, width, rows), BF16),
            pltpu.VMEM((2, SIDE, 2, fh, rows), BF16),
            pltpu.VMEM((2, SIDE, 2, fq, rows), BF16),
            pltpu.VMEM((2, 2, fh, rows), BF16),
            pltpu.VMEM((2, 2, fq, rows), BF16),
            pltpu.VMEM((ZC, labels, wide), BF16),
            pltpu.VMEM((ZC, labels, wide), BF16),
            pltpu.VMEM((ZC, 2, piece // 2, wide), BF16),
            pltpu.VMEM((ZC, 2, far - 1, piece, wide), BF16),
            pltpu.VMEM((2, 1, width), F32),
            pltpu.VMEM((SIDE, 1, width), F32),
            pltpu.VMEM((SIDE, 1, width), F32),
            pltpu.VMEM((depth, 1, width), F32),
            pltpu.VMEM((rows, width), F32),
            pltpu.VMEM((rows, width), F32),
            pltpu.VMEM((rows, 1), F32),
            dma((7,)),
            dma((3,)),
            dma((3,)),
            dma,
            dma((2, len(CHIPS))),
            dma((len(CHIPS),)),
            dma,
            dma((len(CHIPS) // GROUP,)),
            dma,
            dma((2, SIDE, 2)),
            dma((2, SIDE, 2)),
            dma((2, 2)),
            dma((2, 2)),
            dma,
            dma((ZC, 2)),
            dma((ZC, 2, far - 1)),
            dma,
            dma((ZC, 2, far)),
            dma((4,)),
            dma((4,)),
        ],
        compiler_params=pltpu.CompilerParams(
            collective_id=0, has_side_effects=True, vmem_limit_bytes=48 * 1024 * 1024
        ),
    )(
        cluster_sizes,
        *(
            pltpu.with_memory_space_constraint(a, pltpu.HBM)
            for a in (
                hidden_states, ln_gain.reshape(width // 128, 128), beam_ids.T, positive_ids.T,
                head_rows[0], first_moment[0], second_moment[0],
            )
        ),
    )
    whole = pltpu.HBM((1, labels, width), F32)
    *rest, gain_grad = pl.pallas_call(
        store,
        out_shape=(whole, whole, whole, *[pltpu.HBM(r.shape, r.dtype) for r in results[3:]]),
        in_specs=[pl.BlockSpec(memory_space=pl.ANY)] * 5,
        out_specs=(hbm,) * 5,
        scratch_shapes=[dma((5,))],
        compiler_params=pltpu.CompilerParams(vmem_limit_bytes=16 * 1024 * 1024),
    )(*(pltpu.with_memory_space_constraint(r, pltpu.VMEM) for r in results))
    return (*rest, gain_grad.reshape(width))


def solution(mesh):
    in_specs = (
        P(("cluster", "dp"), None),
        P(),
        P(("cluster", "dp"), None),
        P(("cluster", "dp"), None),
        P("cluster"),
        P("cluster", None, None),
        P("cluster", None, None),
        P("cluster", None, None),
    )
    out_specs = (
        P("cluster", None, None),
        P("cluster", None, None),
        P("cluster", None, None),
        P(("cluster", "dp"), None),
        P(),
    )
    return jax.shard_map(shards, mesh=mesh, in_specs=in_specs, out_specs=out_specs, check_vma=False)
```

```python
import functools

import jax
import jax.numpy as jnp
from jax import lax
from jax.experimental import pallas as pl
from jax.experimental.pallas import tpu as pltpu
from jax.sharding import PartitionSpec as P

MESH = pl.DeviceIdType.MESH
F32 = jnp.float32
BF16 = jnp.bfloat16

norm_eps = 1e-05
learn_rate = 0.01
first_decay = 0.9
second_decay = 0.999
adam_eps = 1e-08
second_fix = 0.632304575226

SIDE = 4
PLANE = 32
CHIPS = (
    (0, 0), (1, 0), (0, 1), (3, 0), (0, 3), (2, 0), (0, 2), (1, 1),
    (3, 3), (1, 3), (3, 1), (2, 1), (1, 2), (2, 3), (3, 2), (2, 2),
)
PLACE = {offset: i for i, offset in enumerate(CHIPS)}
GROUPS = ((0, 5), (5, 3), (8, 3), (11, 5))
MOST = max(n for _, n in GROUPS)
ZC = 3


def kernel(
    size_in, hid_in, gain_in, beam_in, pos_in, head_in, first_in, second_in,
    nh_ref, nf_ref, ns_ref, igrad_ref, ggrad_ref,
    hid, gain_v, beam_v, pos_v, head, first, second,
    emb, ids, wh, wt, hg, slope_v, part, from_core, half_in, quart_in, half_in2, quart_in2,
    hgb, hgf, zq, zh, gc, gx, gy, gz, egrad, normed_v, inverse_v,
    in_sem, ids_send, ids_recv, ag_send, ag_recv, core_recv,
    core_send, rs_core, rs_send, rs_h, rs_q, rs_h2, rs_q2,
    z_send, z_q, z_h, zg_send, zg, g_send, g_recv,
):
    c = lax.axis_index("cluster")
    z = lax.axis_index("dp")
    depth = lax.axis_size("dp")
    rows, width = hid.shape
    labels = head.shape[0]
    beam = beam_v.shape[0]
    x, y, k = c // (2 * SIDE), lax.rem(c // 2, SIDE), lax.rem(c, 2)
    sibling = (c + 1 - 2 * k, z)

    def dev(dx, dy):
        return ((lax.rem(x + dx, SIDE) * SIDE + lax.rem(y + dy, SIDE)) * 2 + k, z)

    def turned(t, du, dv):
        du, dv = du % SIDE, dv % SIDE
        return (du, dv) if t == 0 else (dv, du)

    def copy(src, dst, send, recv, device):
        return pltpu.make_async_remote_copy(
            src_ref=src, dst_ref=dst, send_sem=send, recv_sem=recv, device_id=device, device_id_type=MESH
        )

    def arrived(dst, recv):
        copy(dst, dst, recv, recv, sibling).wait_recv()

    def sent(src, send):
        copy(src, src, send, send, sibling).wait_send()

    loads = [
        pltpu.make_async_copy(src, dst, in_sem.at[i])
        for i, (src, dst) in enumerate(
            (
                (beam_in, beam_v), (pos_in, pos_v), (hid_in, hid), (gain_in, gain_v),
                (head_in, head), (first_in, first), (second_in, second),
            )
        )
    ]
    for load in loads:
        load.start()

    barrier = pltpu.get_barrier_semaphore()
    pl.semaphore_signal(barrier, inc=1, device_id=sibling, device_id_type=MESH)
    for i in range(1, SIDE):
        pl.semaphore_signal(barrier, inc=1, device_id=dev(i, 0), device_id_type=MESH)
        pl.semaphore_signal(barrier, inc=1, device_id=dev(0, i), device_id_type=MESH)

    def greet(i, _):
        pl.semaphore_signal(barrier, inc=1, device_id=(c, lax.rem(z + i, depth)), device_id_type=MESH)
        return _

    lax.fori_loop(1, depth, greet, 0)

    half, quart = rows // 2, rows // 4

    def push(t, at, lo, n, tu, tv):
        du, dv = turned(t, *CHIPS[at])
        to = PLACE[turned(t, du - tu, dv - tv)]
        src, dst = emb.at[2 * at + k, pl.ds(lo, n)], emb.at[2 * to + k, pl.ds(lo, n)]
        copy(src, dst, ag_send, ag_recv.at[t, to], dev(*turned(t, tu, tv))).start()

    def half_in_hand(t, du, dv):
        at, lo = PLACE[turned(t, du, dv)], t * half
        if at > 0:
            arrived(emb.at[2 * at + k, pl.ds(lo, half)], ag_recv.at[t, at])
        if dv == 0:
            if du == 0:
                push(t, at, lo, half, 1, 0)
                push(t, at, lo, half, -1, 0)
            elif du == 3:
                push(t, at, lo, quart, 1, 0)
            elif du == 1:
                push(t, at, lo + quart, quart, -1, 0)
            push(t, at, lo, half, 0, 1)
            push(t, at, lo, half, 0, -1)
        elif dv == 3:
            push(t, at, lo, quart, 0, 1)
        elif dv == 1:
            push(t, at, lo + quart, quart, 0, -1)

    def event(*offsets, whole=()):
        for du, dv in offsets:
            for t in range(2):
                half_in_hand(t, du, dv)
        for offset in whole:
            mine = emb.at[2 * PLACE[offset] + k]
            copy(mine, mine, ag_send, core_recv.at[PLACE[offset]], sibling).start()

    for load in loads[:4]:
        load.wait()
    gain = jnp.concatenate([gain_v[i : i + 1, :] for i in range(width // 128)], axis=1)
    values = hid[...].astype(F32)
    center = jnp.mean(values, axis=1, keepdims=True)
    spread = jnp.mean(jnp.square(values - center), axis=1, keepdims=True)
    inverse = lax.rsqrt(spread + norm_eps)
    normed = (values - center) * inverse
    normed_v[...] = normed
    inverse_v[...] = inverse
    emb[k] = (normed * gain).astype(BF16)
    ids[x, y, k] = jnp.concatenate([beam_v[...], pos_v[...]], axis=0).astype(jnp.int16)
    pl.semaphore_wait(barrier, 1 + 2 * (SIDE - 1) + depth - 1)

    event((0, 0), whole=((0, 0),))
    for i in range(1, SIDE):
        own = ids.at[x, y, k]
        copy(own, own, ids_send.at[0], ids_recv.at[0], dev(i, 0)).start()

    loads[4].wait()
    wh[...] = (head[...].astype(BF16) * 0.5).astype(BF16)
    for i in range(width // 128):
        cols = pl.ds(i * 128, 128)
        wt[cols, :] = head[:, cols].T.astype(BF16)
    hg[...] = jnp.zeros_like(hg)
    size = size_in[0]

    arrived(ids.at[pl.ds(0, SIDE - 1), y, k], ids_recv.at[0])
    for i in range(1, SIDE):
        own = ids.at[:, y, k]
        copy(own, own, ids_send.at[1], ids_recv.at[1], dev(0, i)).start()
    event((1, 0), (3, 0))
    event((0, 1), (0, 3), whole=((1, 0), (0, 1), (3, 0), (0, 3)))
    arrived(ids.at[:, pl.ds(0, SIDE - 1), k], ids_recv.at[1])
    own = ids.at[:, :, k]
    copy(own, own, ids_send.at[2], ids_recv.at[2], sibling).start()

    def chips_of(g):
        first, n = GROUPS[g]
        return range(first, first + n)

    def block_of(g):
        first, n = GROUPS[g]
        return emb[pl.ds(2 * first, 2 * n)].reshape(2 * n * rows, width)

    def slope_of(g):
        return slope_v[:, : 2 * GROUPS[g][1] * rows]

    def score(g):
        label, limit = [], []
        many = 2 * GROUPS[g][1] * rows
        for at in chips_of(g):
            arrived(emb.at[2 * at + 1 - k], core_recv.at[at])
            dx, dy = CHIPS[at]
            for s in range(2):
                own = ids[lax.rem(x + dx, SIDE), lax.rem(y + dy, SIDE), s].astype(jnp.int32)
                match = own[0:beam] == c
                place = lax.broadcasted_iota(jnp.int32, (beam, rows), 0)
                place = jnp.sum(jnp.where(match, place, 0), axis=0, keepdims=True)
                chosen = jnp.max(jnp.where(match, 1, 0), axis=0, keepdims=True)
                label.append(own[beam:] - place * labels)
                limit.append(chosen * size)
        label = jnp.concatenate(label, axis=1)
        limit = jnp.concatenate(limit, axis=1)
        logits = lax.dot_general(wh[...], block_of(g), (((1,), (1,)), ((), ())), preferred_element_type=F32)
        word = lax.shift_right_arithmetic(label, 5)
        bit = lax.shift_left(jnp.ones_like(label), label & 31)
        words = lax.broadcasted_iota(jnp.int32, (labels // 32, many), 0)
        bits = jnp.zeros_like(words)
        for p in range(label.shape[0]):
            bits = bits | jnp.where(word[p : p + 1] == words, bit[p : p + 1], 0)
        step = 0.5 / beam
        for i in range(labels // 32):
            slot = lax.broadcasted_iota(jnp.int32, (32, many), 0)
            hit = lax.shift_left(jnp.broadcast_to(bits[i : i + 1], (32, many)), 31 - slot) < 0
            slope = step * jnp.tanh(logits[32 * i : 32 * i + 32]) + jnp.where(hit, -step, step)
            slope = jnp.where(slot + 32 * i < limit, slope, 0.0)
            slope_v[pl.ds(32 * i, 32), :many] = slope.astype(BF16)

    def gather_head(g):
        hg[...] += jnp.dot(slope_of(g), block_of(g), preferred_element_type=F32)

    def back(g):
        grads = jnp.dot(wt[...], slope_of(g), preferred_element_type=F32).astype(BF16)
        for q, at in enumerate(chips_of(g)):
            for s in range(2):
                i = 2 * q + s
                part[at, s] = grads[:, i * rows : (i + 1) * rows]
        there = pl.ds(*GROUPS[g])
        copy(part.at[there, 1 - k], from_core.at[there], core_send, rs_core.at[g], sibling).start()

    def join(g):
        arrived(from_core.at[pl.ds(*GROUPS[g])], rs_core.at[g])
        for at in chips_of(g):
            part[at, k] += from_core[at]

    arrived(ids.at[:, :, k], ids_recv.at[2])
    score(0)
    gather_head(0)
    event((2, 0))
    back(0)
    event((1, 1), whole=((1, 1),))
    event((0, 2), whole=((2, 0), (0, 2)))
    score(1)
    event((3, 3), whole=((3, 3),))
    event((1, 3), (3, 1), whole=((1, 3), (3, 1)))
    gather_head(1)
    back(1)
    join(0)
    score(2)
    event((2, 1), (2, 3))
    gather_head(2)
    back(2)
    join(1)
    event((1, 2), (3, 2), whole=((2, 1), (1, 2), (2, 3), (3, 2)))
    event((2, 2), whole=((2, 2),))
    score(3)
    gather_head(3)

    piece = labels // depth
    part_z = piece // 2
    far = depth // 2
    wide = width // ZC

    def at_z(i):
        return lax.rem(z + i + depth, depth)

    def rows_z(i, lo=0, n=piece):
        return pl.ds(pl.multiple_of(at_z(i) * piece + lo, part_z), n)

    def z_first(h):
        hgb[h] = hg[:, h * wide : (h + 1) * wide].astype(BF16)
        for s in range(2):
            src = hgb.at[h, rows_z(far, s * part_z, part_z)]
            copy(src, zq.at[h, s], z_send, z_q.at[h, s], (c, at_z(1 - 2 * s))).start()

    def z_next(h, i):
        for s in range(2):
            way = 1 - 2 * s
            own = rows_z(way * (far - 1 - i))
            if i == 0:
                arrived(zq.at[h, s], z_q.at[h, s])
                mid = rows_z(way * (far - 1), s * part_z, part_z)
                hgb[h, mid] += zq[h, s]
            else:
                arrived(zh.at[h, s, i - 1], z_h.at[h, s, i - 1])
                hgb[h, own] += zh[h, s, i - 1]
            copy(hgb.at[h, own], zh.at[h, s, i], z_send, z_h.at[h, s, i], (c, at_z(way))).start()

    def adam(h, at):
        cols = pl.ds(h * wide, wide)
        grad = hgf[h, at].astype(F32)
        new_first = first_decay * first[at, cols] + (1.0 - first_decay) * grad
        new_second = second_decay * second[at, cols] + (1.0 - second_decay) * grad * grad
        nf_ref[at, cols] = new_first
        ns_ref[at, cols] = new_second
        step_size = new_first / (jnp.sqrt(new_second * (1.0 / second_fix)) + adam_eps)
        nh_ref[at, cols] = head[at, cols] - learn_rate * step_size

    def z_last(h):
        total = hgb[h, rows_z(0)].astype(F32)
        for s in range(2):
            arrived(zh.at[h, s, far - 2], z_h.at[h, s, far - 2])
            total += zh[h, s, far - 2].astype(F32)
        hgf[h, rows_z(0)] = total.astype(BF16)
        for s in range(2):
            own = hgf.at[h, rows_z(0)]
            copy(own, own, zg_send, zg.at[h, s, 0], (c, at_z(1 - 2 * s))).start()

    def z_spread(h, i):
        for s in range(2):
            way = 1 - 2 * s
            own = hgf.at[h, rows_z(-way * i)]
            arrived(own, zg.at[h, s, i - 1])
            if i == far - 1:
                own = hgf.at[h, rows_z(-way * i, s * part_z, part_z)]
            copy(own, own, zg_send, zg.at[h, s, i], (c, at_z(way))).start()

    def z_adam(h, i):
        adam(h, rows_z(i))
        adam(h, rows_z(-i))

    def z_end(h):
        for s in range(2):
            arrived(hgf.at[h, rows_z(far, s * part_z, part_z)], zg.at[h, s, far - 1])
        adam(h, rows_z(far))

    fh, fq = width // 2, width // 4

    def feats(t, lo, n):
        return pl.ds(t * fh + lo, n)

    def dest(t, du, dv):
        return PLACE[turned(t, du, dv)]

    def v_first(t, du):
        for s in range(2):
            src = part.at[dest(t, du, 2), k, feats(t, s * fq, fq)]
            to = dev(*turned(t, 0, 1 - 2 * s))
            copy(src, quart_in.at[t, du, s], rs_send, rs_q.at[t, du, s], to).start()

    def v_next(t, du):
        for s in range(2):
            arrived(quart_in.at[t, du, s], rs_q.at[t, du, s])
            to = dest(t, du, 1 - 2 * s)
            part[to, k, feats(t, s * fq, fq)] += quart_in[t, du, s]
            src = part.at[to, k, feats(t, 0, fh)]
            copy(src, half_in.at[t, du, s], rs_send, rs_h.at[t, du, s], dev(*turned(t, 0, 1 - 2 * s))).start()

    def v_last(t, du):
        to = dest(t, du, 0)
        for s in range(2):
            arrived(half_in.at[t, du, s], rs_h.at[t, du, s])
        total = part[to, k, feats(t, 0, fh)].astype(F32)
        total += half_in[t, du, 0].astype(F32) + half_in[t, du, 1].astype(F32)
        part[to, k, feats(t, 0, fh)] = total.astype(BF16)

    def u_first(t):
        for s in range(2):
            src = part.at[dest(t, 2, 0), k, feats(t, s * fq, fq)]
            copy(src, quart_in2.at[t, s], rs_send, rs_q2.at[t, s], dev(*turned(t, 1 - 2 * s, 0))).start()

    def u_next(t):
        for s in range(2):
            arrived(quart_in2.at[t, s], rs_q2.at[t, s])
            to = dest(t, 1 - 2 * s, 0)
            part[to, k, feats(t, s * fq, fq)] += quart_in2[t, s]
            src = part.at[to, k, feats(t, 0, fh)]
            copy(src, half_in2.at[t, s], rs_send, rs_h2.at[t, s], dev(*turned(t, 1 - 2 * s, 0))).start()

    def u_last(t):
        for s in range(2):
            arrived(half_in2.at[t, s], rs_h2.at[t, s])
        total = part[0, k, feats(t, 0, fh)].astype(F32)
        total += half_in2[t, 0].astype(F32) + half_in2[t, 1].astype(F32)
        egrad[:, t * fh : (t + 1) * fh] = total.T

    def g_first():
        gc[k] = jnp.sum(wh[...].astype(F32) * hg[...], axis=0, keepdims=True) * 2.0
        copy(gc.at[k], gc.at[k], g_send.at[0], g_recv.at[0], sibling).start()

    def g_x():
        arrived(gc.at[0], g_recv.at[0])
        gx[x] = gc[0] + gc[1]
        for i in range(1, SIDE):
            copy(gx.at[x], gx.at[x], g_send.at[1], g_recv.at[1], dev(i, 0)).start()

    def g_y():
        arrived(gx.at[pl.ds(0, SIDE - 1)], g_recv.at[1])
        gy[y] = jnp.sum(gx[...], axis=0)
        for i in range(1, SIDE):
            copy(gy.at[y], gy.at[y], g_send.at[2], g_recv.at[2], dev(0, i)).start()

    def g_z():
        arrived(gy.at[pl.ds(0, SIDE - 1)], g_recv.at[2])
        gz[z] = jnp.sum(gy[...], axis=0)

        def send(i, _):
            copy(gz.at[z], gz.at[z], g_send.at[3], g_recv.at[3], (c, at_z(i))).start()
            return _

        lax.fori_loop(1, depth, send, 0)

    def g_last():
        arrived(gz.at[pl.ds(0, depth - 1)], g_recv.at[3])
        total = jnp.sum(gz[...], axis=0) / gain
        for i in range(width // 128):
            ggrad_ref[i : i + 1, :] = total[:, i * 128 : (i + 1) * 128]

    chunks = range(ZC)
    for h in chunks:
        z_first(h)
    back(3)
    join(2)
    g_first()
    for h in chunks:
        z_next(h, 0)
    join(3)
    for du in (2, 1, 3, 0):
        for t in range(2):
            v_first(t, du)
    g_x()
    for h in chunks:
        z_next(h, 1)
    for t in range(2):
        v_next(t, 2)
    for t in range(2):
        v_next(t, 1)
    for h in chunks[: ZC // 2]:
        z_next(h, 2)
    for t in range(2):
        v_next(t, 3)
    for h in chunks[ZC // 2 :]:
        z_next(h, 2)
    for t in range(2):
        v_next(t, 0)
    g_y()
    for h in chunks[: ZC // 2]:
        z_last(h)
    for t in range(2):
        v_last(t, 2)
        u_first(t)
    for h in chunks[ZC // 2 :]:
        z_last(h)
    loads[5].wait()
    loads[6].wait()
    for t in range(2):
        v_last(t, 1)
    for h in chunks:
        z_spread(h, 1)
    g_z()
    for t in range(2):
        v_last(t, 3)
    for t in range(2):
        u_next(t)
    for h in chunks:
        z_spread(h, 2)
        adam(h, rows_z(0))
    for t in range(2):
        v_last(t, 0)
    for h in chunks:
        z_adam(h, 1)
    for h in chunks:
        z_spread(h, 3)
    for t in range(2):
        u_last(t)
    for h in chunks:
        z_adam(h, 2)

    scaled = egrad[...] * gain
    normed = normed_v[...]
    first_mean = jnp.mean(scaled, axis=1, keepdims=True)
    second_mean = jnp.mean(scaled * normed, axis=1, keepdims=True)
    igrad_ref[...] = ((scaled - first_mean - normed * second_mean) * inverse_v[...]).astype(BF16)

    for h in chunks:
        z_adam(h, 3)
    g_last()
    for h in chunks:
        z_end(h)

    sent(emb.at[pl.ds(0, PLANE - 1)], ag_send)
    sent(from_core, core_send)
    sent(from_core.at[pl.ds(0, PLANE // 2 - 1)], rs_send)
    sent(ids.at[pl.ds(0, SIDE - 1), y, k], ids_send.at[0])
    sent(ids.at[:, pl.ds(0, SIDE - 1), k], ids_send.at[1])
    sent(ids.at[:, :, k], ids_send.at[2])
    sent(gc.at[0], g_send.at[0])
    sent(gx.at[pl.ds(0, SIDE - 1)], g_send.at[1])
    sent(gy.at[pl.ds(0, SIDE - 1)], g_send.at[2])
    sent(gz.at[pl.ds(0, depth - 1)], g_send.at[3])
    sent(hgb.at[:, pl.ds(0, labels - piece)], z_send)
    sent(hgf.at[:, pl.ds(0, labels - piece)], zg_send)


def store(nh, nf, ns, igrad, ggrad, nh_out, nf_out, ns_out, igrad_out, ggrad_out, sem):
    pairs = ((nh, nh_out.at[0]), (nf, nf_out.at[0]), (ns, ns_out.at[0]), (igrad, igrad_out), (ggrad, ggrad_out))
    copies = [pltpu.make_async_copy(src, dst, sem.at[i]) for i, (src, dst) in enumerate(pairs)]
    for copy in copies:
        copy.start()
    for copy in copies:
        copy.wait()


def shards(
    hidden_states,
    ln_gain,
    beam_ids,
    positive_ids,
    cluster_sizes,
    head_rows,
    first_moment,
    second_moment,
):
    rows, width = hidden_states.shape
    labels = head_rows.shape[1]
    beam, pos = beam_ids.shape[1], positive_ids.shape[1]
    depth = lax.axis_size("dp")
    vmem = pl.BlockSpec(memory_space=pltpu.VMEM)
    hbm = pl.BlockSpec(memory_space=pltpu.HBM)
    fh, fq, piece, far, wide = width // 2, width // 4, labels // depth, depth // 2, width // ZC
    dma = pltpu.SemaphoreType.DMA
    head_shape = pltpu.VMEM((labels, width), F32)
    results = pl.pallas_call(
        kernel,
        out_shape=(
            head_shape,
            head_shape,
            head_shape,
            pltpu.VMEM((rows, width), BF16),
            pltpu.VMEM((width // 128, 128), F32),
        ),
        in_specs=[pl.BlockSpec(memory_space=pltpu.SMEM)] + [hbm] * 7,
        out_specs=(vmem,) * 5,
        scratch_shapes=[
            pltpu.VMEM((rows, width), BF16),
            pltpu.VMEM((width // 128, 128), F32),
            pltpu.VMEM((beam, rows), jnp.int32),
            pltpu.VMEM((pos, rows), jnp.int32),
            pltpu.VMEM((labels, width), F32),
            pltpu.VMEM((labels, width), F32),
            pltpu.VMEM((labels, width), F32),
            pltpu.VMEM((PLANE, rows, width), BF16),
            pltpu.VMEM((SIDE, SIDE, 2, beam + pos, rows), jnp.int16),
            pltpu.VMEM((labels, width), BF16),
            pltpu.VMEM((width, labels), BF16),
            pltpu.VMEM((labels, width), F32),
            pltpu.VMEM((labels, 2 * MOST * rows), BF16),
            pltpu.VMEM((PLANE // 2, 2, width, rows), BF16),
            pltpu.VMEM((PLANE // 2, width, rows), BF16),
            pltpu.VMEM((2, SIDE, 2, fh, rows), BF16),
            pltpu.VMEM((2, SIDE, 2, fq, rows), BF16),
            pltpu.VMEM((2, 2, fh, rows), BF16),
            pltpu.VMEM((2, 2, fq, rows), BF16),
            pltpu.VMEM((ZC, labels, wide), BF16),
            pltpu.VMEM((ZC, labels, wide), BF16),
            pltpu.VMEM((ZC, 2, piece // 2, wide), BF16),
            pltpu.VMEM((ZC, 2, far - 1, piece, wide), BF16),
            pltpu.VMEM((2, 1, width), F32),
            pltpu.VMEM((SIDE, 1, width), F32),
            pltpu.VMEM((SIDE, 1, width), F32),
            pltpu.VMEM((depth, 1, width), F32),
            pltpu.VMEM((rows, width), F32),
            pltpu.VMEM((rows, width), F32),
            pltpu.VMEM((rows, 1), F32),
            dma((7,)),
            dma((3,)),
            dma((3,)),
            dma,
            dma((2, len(CHIPS))),
            dma((len(CHIPS),)),
            dma,
            dma((len(GROUPS),)),
            dma,
            dma((2, SIDE, 2)),
            dma((2, SIDE, 2)),
            dma((2, 2)),
            dma((2, 2)),
            dma,
            dma((ZC, 2)),
            dma((ZC, 2, far - 1)),
            dma,
            dma((ZC, 2, far)),
            dma((4,)),
            dma((4,)),
        ],
        compiler_params=pltpu.CompilerParams(
            collective_id=0, has_side_effects=True, vmem_limit_bytes=48 * 1024 * 1024
        ),
    )(
        cluster_sizes,
        *(
            pltpu.with_memory_space_constraint(a, pltpu.HBM)
            for a in (
                hidden_states, ln_gain.reshape(width // 128, 128), beam_ids.T, positive_ids.T,
                head_rows[0], first_moment[0], second_moment[0],
            )
        ),
    )
    whole = pltpu.HBM((1, labels, width), F32)
    *rest, gain_grad = pl.pallas_call(
        store,
        out_shape=(whole, whole, whole, *[pltpu.HBM(r.shape, r.dtype) for r in results[3:]]),
        in_specs=[pl.BlockSpec(memory_space=pl.ANY)] * 5,
        out_specs=(hbm,) * 5,
        scratch_shapes=[dma((5,))],
        compiler_params=pltpu.CompilerParams(vmem_limit_bytes=16 * 1024 * 1024),
    )(*(pltpu.with_memory_space_constraint(r, pltpu.VMEM) for r in results))
    return (*rest, gain_grad.reshape(width))


def solution(mesh):
    in_specs = (
        P(("cluster", "dp"), None),
        P(),
        P(("cluster", "dp"), None),
        P(("cluster", "dp"), None),
        P("cluster"),
        P("cluster", None, None),
        P("cluster", None, None),
        P("cluster", None, None),
    )
    out_specs = (
        P("cluster", None, None),
        P("cluster", None, None),
        P("cluster", None, None),
        P(("cluster", "dp"), None),
        P(),
    )
    return jax.shard_map(shards, mesh=mesh, in_specs=in_specs, out_specs=out_specs, check_vma=False)
```

```python
import functools

import jax
import jax.numpy as jnp
from jax import lax
from jax.experimental import pallas as pl
from jax.experimental.pallas import tpu as pltpu
from jax.sharding import PartitionSpec as P

MESH = pl.DeviceIdType.MESH
F32 = jnp.float32
BF16 = jnp.bfloat16

norm_eps = 1e-05
learn_rate = 0.01
first_decay = 0.9
second_decay = 0.999
adam_eps = 1e-08
second_fix = 0.632304575226

SIDE = 4
PLANE = 32
CHIPS = (
    (0, 0), (1, 0), (0, 1), (3, 0), (0, 3), (2, 0), (0, 2), (1, 1),
    (3, 3), (1, 3), (3, 1), (2, 1), (1, 2), (2, 3), (3, 2), (2, 2),
)
PLACE = {offset: i for i, offset in enumerate(CHIPS)}
GROUPS = ((0, 5), (5, 3), (8, 3), (11, 5))
MOST = max(n for _, n in GROUPS)
ZC = 3


def kernel(
    size_in, hid_in, gain_in, beam_in, pos_in, head_in, first_in, second_in,
    nh_ref, nf_ref, ns_ref, igrad_ref, ggrad_ref,
    hid, gain_v, beam_v, pos_v, head, first, second,
    emb, ids, wh, wt, hg, slope_v, part, from_core, half_in, quart_in, half_in2, quart_in2,
    hgb, hgf, zq, zh, gp, gc, gz, egrad, normed_v, inverse_v,
    in_sem, ids_send, ids_recv, ag_send, ag_recv, core_recv,
    core_send, rs_core, rs_send, rs_h, rs_q, rs_h2, rs_q2,
    z_send, z_q, z_h, zg_send, zg, g_send, g_recv,
):
    c = lax.axis_index("cluster")
    z = lax.axis_index("dp")
    depth = lax.axis_size("dp")
    rows, width = hid.shape
    labels = head.shape[0]
    beam = beam_v.shape[0]
    x, y, k = c // (2 * SIDE), lax.rem(c // 2, SIDE), lax.rem(c, 2)
    sibling = (c + 1 - 2 * k, z)

    def dev(dx, dy):
        return ((lax.rem(x + dx, SIDE) * SIDE + lax.rem(y + dy, SIDE)) * 2 + k, z)

    def chip_peer(i):
        return (lax.rem(c // 2 + i, SIDE * SIDE) * 2 + k, z)

    def turned(t, du, dv):
        du, dv = du % SIDE, dv % SIDE
        return (du, dv) if t == 0 else (dv, du)

    def copy(src, dst, send, recv, device):
        return pltpu.make_async_remote_copy(
            src_ref=src, dst_ref=dst, send_sem=send, recv_sem=recv, device_id=device, device_id_type=MESH
        )

    def arrived(dst, recv):
        copy(dst, dst, recv, recv, sibling).wait_recv()

    def sent(src, send):
        copy(src, src, send, send, sibling).wait_send()

    loads = [
        pltpu.make_async_copy(src, dst, in_sem.at[i])
        for i, (src, dst) in enumerate(
            (
                (beam_in, beam_v), (pos_in, pos_v), (hid_in, hid), (gain_in, gain_v),
                (head_in, head), (first_in, first), (second_in, second),
            )
        )
    ]
    for load in loads:
        load.start()

    barrier = pltpu.get_barrier_semaphore()
    pl.semaphore_signal(barrier, inc=1, device_id=sibling, device_id_type=MESH)

    def greet_plane(i, _):
        pl.semaphore_signal(barrier, inc=1, device_id=chip_peer(i), device_id_type=MESH)
        return _

    def greet(i, _):
        pl.semaphore_signal(barrier, inc=1, device_id=(c, lax.rem(z + i, depth)), device_id_type=MESH)
        return _

    lax.fori_loop(1, SIDE * SIDE, greet_plane, 0)
    lax.fori_loop(1, depth, greet, 0)

    half, quart = rows // 2, rows // 4

    def push(t, at, lo, n, tu, tv):
        du, dv = turned(t, *CHIPS[at])
        to = PLACE[turned(t, du - tu, dv - tv)]
        src, dst = emb.at[2 * at + k, pl.ds(lo, n)], emb.at[2 * to + k, pl.ds(lo, n)]
        copy(src, dst, ag_send, ag_recv.at[t, to], dev(*turned(t, tu, tv))).start()

    def half_in_hand(t, du, dv, early=True, late=True):
        at, lo = PLACE[turned(t, du, dv)], t * half
        if at > 0 and early:
            arrived(emb.at[2 * at + k, pl.ds(lo, half)], ag_recv.at[t, at])
        if dv == 0:
            if not early:
                pass
            elif du == 0:
                push(t, at, lo, half, 1, 0)
                push(t, at, lo, half, -1, 0)
            elif du == 3:
                push(t, at, lo, quart, 1, 0)
            elif du == 1:
                push(t, at, lo + quart, quart, -1, 0)
            if late:
                push(t, at, lo, half, 0, 1)
                push(t, at, lo, half, 0, -1)
        elif dv == 3:
            push(t, at, lo, quart, 0, 1)
        elif dv == 1:
            push(t, at, lo + quart, quart, 0, -1)

    def event(*offsets, whole=()):
        for du, dv in offsets:
            for t in range(2):
                half_in_hand(t, du, dv)
        for offset in whole:
            mine = emb.at[2 * PLACE[offset] + k]
            copy(mine, mine, ag_send, core_recv.at[PLACE[offset]], sibling).start()

    for load in loads[:4]:
        load.wait()
    gain = jnp.concatenate([gain_v[i : i + 1, :] for i in range(width // 128)], axis=1)
    values = hid[...].astype(F32)
    center = jnp.mean(values, axis=1, keepdims=True)
    spread = jnp.mean(jnp.square(values - center), axis=1, keepdims=True)
    inverse = lax.rsqrt(spread + norm_eps)
    normed = (values - center) * inverse
    normed_v[...] = normed
    inverse_v[...] = inverse
    emb[k] = (normed * gain).astype(BF16)
    ids[k, c // 2] = jnp.concatenate([beam_v[...], pos_v[...]], axis=0).astype(jnp.int16)
    pl.semaphore_wait(barrier, SIDE * SIDE + depth - 1)

    def send_ids(i, _):
        own = ids.at[k, c // 2]
        copy(own, own, ids_send.at[0], ids_recv.at[0], chip_peer(i)).start()
        return _

    lax.fori_loop(1, SIDE * SIDE, send_ids, 0)
    event((0, 0), whole=((0, 0),))

    loads[4].wait()
    wh[...] = (head[...].astype(BF16) * 0.5).astype(BF16)
    for i in range(width // 128):
        cols = pl.ds(i * 128, 128)
        wt[cols, :] = head[:, cols].T.astype(BF16)
    hg[...] = jnp.zeros_like(hg)
    size = size_in[0]

    for early in (True, False):
        for du in (1, 3):
            for t in range(2):
                half_in_hand(t, du, 0, early, not early)
    arrived(ids.at[k, pl.ds(0, SIDE * SIDE - 1)], ids_recv.at[0])
    copy(ids.at[k], ids.at[k], ids_send.at[1], ids_recv.at[1], sibling).start()
    event((0, 1), (0, 3), whole=((1, 0), (0, 1), (3, 0), (0, 3)))
    def chips_of(g):
        first, n = GROUPS[g]
        return range(first, first + n)

    def block_of(g):
        first, n = GROUPS[g]
        return emb[pl.ds(2 * first, 2 * n)].reshape(2 * n * rows, width)

    def slope_of(g):
        return slope_v[:, : 2 * GROUPS[g][1] * rows]

    def score(g):
        label, limit = [], []
        many = 2 * GROUPS[g][1] * rows
        for at in chips_of(g):
            arrived(emb.at[2 * at + 1 - k], core_recv.at[at])
            dx, dy = CHIPS[at]
            for s in range(2):
                own = ids[s, lax.rem(x + dx, SIDE) * SIDE + lax.rem(y + dy, SIDE)].astype(jnp.int32)
                match = own[0:beam] == c
                place = lax.broadcasted_iota(jnp.int32, (beam, rows), 0)
                place = jnp.sum(jnp.where(match, place, 0), axis=0, keepdims=True)
                chosen = jnp.max(jnp.where(match, 1, 0), axis=0, keepdims=True)
                label.append(own[beam:] - place * labels)
                limit.append(chosen * size)
        label = jnp.concatenate(label, axis=1)
        limit = jnp.concatenate(limit, axis=1)
        logits = lax.dot_general(wh[...], block_of(g), (((1,), (1,)), ((), ())), preferred_element_type=F32)
        word = lax.shift_right_arithmetic(label, 5)
        bit = lax.shift_left(jnp.ones_like(label), label & 31)
        words = lax.broadcasted_iota(jnp.int32, (labels // 32, many), 0)
        bits = jnp.zeros_like(words)
        for p in range(label.shape[0]):
            bits = bits | jnp.where(word[p : p + 1] == words, bit[p : p + 1], 0)
        step = 0.5 / beam
        for i in range(labels // 32):
            slot = lax.broadcasted_iota(jnp.int32, (32, many), 0)
            hit = lax.shift_left(jnp.broadcast_to(bits[i : i + 1], (32, many)), 31 - slot) < 0
            slope = step * jnp.tanh(logits[32 * i : 32 * i + 32]) + jnp.where(hit, -step, step)
            slope = jnp.where(slot + 32 * i < limit, slope, 0.0)
            slope_v[pl.ds(32 * i, 32), :many] = slope.astype(BF16)

    def gather_head(g, lo=0, n=width):
        cols = pl.ds(lo, n)
        block = emb[pl.ds(2 * GROUPS[g][0], 2 * GROUPS[g][1]), :, cols].reshape(2 * GROUPS[g][1] * rows, n)
        hg[:, cols] += jnp.dot(slope_of(g), block, preferred_element_type=F32)

    def back(g):
        grads = jnp.dot(wt[...], slope_of(g), preferred_element_type=F32).astype(BF16)
        for q, at in enumerate(chips_of(g)):
            for s in range(2):
                i = 2 * q + s
                part[at, s] = grads[:, i * rows : (i + 1) * rows]
        there = pl.ds(*GROUPS[g])
        copy(part.at[there, 1 - k], from_core.at[there], core_send, rs_core.at[g], sibling).start()

    def join(g):
        arrived(from_core.at[pl.ds(*GROUPS[g])], rs_core.at[g])
        for at in chips_of(g):
            part[at, k] += from_core[at]

    arrived(ids.at[1 - k], ids_recv.at[1])
    score(0)
    gather_head(0)
    event((2, 0))
    back(0)
    event((1, 1), whole=((1, 1),))
    event((0, 2), whole=((2, 0), (0, 2)))
    score(1)
    event((3, 3), whole=((3, 3),))
    event((1, 3), (3, 1), whole=((1, 3), (3, 1)))
    gather_head(1)
    back(1)
    join(0)
    score(2)
    event((2, 1), (2, 3))
    gather_head(2)
    back(2)
    join(1)
    event((1, 2), (3, 2), whole=((2, 1), (1, 2), (2, 3), (3, 2)))
    event((2, 2), whole=((2, 2),))
    score(3)

    piece = labels // depth
    part_z = piece // 2
    far = depth // 2
    wide = width // ZC

    def at_z(i):
        return lax.rem(z + i + depth, depth)

    def rows_z(i, lo=0, n=piece):
        return pl.ds(pl.multiple_of(at_z(i) * piece + lo, part_z), n)

    def z_first(h):
        hgb[h] = hg[:, h * wide : (h + 1) * wide].astype(BF16)
        for s in range(2):
            way = 1 - 2 * s
            src = hgb.at[h, rows_z(far, s * part_z, part_z)]
            copy(src, zq.at[h, s], z_send, z_q.at[h, s], (c, at_z(way))).start()
        for s in range(2):
            way = 1 - 2 * s
            copy(hgb.at[h, rows_z(2 * way)], zh.at[h, s, 0], z_send, z_h.at[h, s, 0], (c, at_z(way))).start()

    def z_second(h):
        for s in range(2):
            way = 1 - 2 * s
            arrived(zq.at[h, s], z_q.at[h, s])
            hgb[h, rows_z(3 * way, s * part_z, part_z)] += zq[h, s]
            copy(hgb.at[h, rows_z(3 * way)], zh.at[h, s, 1], z_send, z_h.at[h, s, 1], (c, at_z(2 * way))).start()

    def z_third(h):
        for s in range(2):
            way = 1 - 2 * s
            arrived(zh.at[h, s, 0], z_h.at[h, s, 0])
            arrived(zh.at[h, s, 1], z_h.at[h, s, 1])
            total = hgb[h, rows_z(way)].astype(F32) + zh[h, s, 0].astype(F32) + zh[h, s, 1].astype(F32)
            hgb[h, rows_z(way)] = total.astype(BF16)
            copy(hgb.at[h, rows_z(way)], zh.at[h, s, 2], z_send, z_h.at[h, s, 2], (c, at_z(way))).start()

    def adam(h, at):
        cols = pl.ds(h * wide, wide)
        grad = hgf[h, at].astype(F32)
        new_first = first_decay * first[at, cols] + (1.0 - first_decay) * grad
        new_second = second_decay * second[at, cols] + (1.0 - second_decay) * grad * grad
        nf_ref[at, cols] = new_first
        ns_ref[at, cols] = new_second
        step_size = new_first / (jnp.sqrt(new_second * (1.0 / second_fix)) + adam_eps)
        nh_ref[at, cols] = head[at, cols] - learn_rate * step_size

    def z_last(h):
        total = hgb[h, rows_z(0)].astype(F32)
        for s in range(2):
            arrived(zh.at[h, s, 2], z_h.at[h, s, 2])
            total += zh[h, s, 2].astype(F32)
        hgf[h, rows_z(0)] = total.astype(BF16)
        own = hgf.at[h, rows_z(0)]
        for i in (2, 1):
            for s in range(2):
                copy(own, own, zg_send, zg.at[h, s, i - 1], (c, at_z(i - 2 * i * s))).start()

    def z_spread(h):
        for s in range(2):
            way = 1 - 2 * s
            own = hgf.at[h, rows_z(-2 * way)]
            arrived(own, zg.at[h, s, 1])
            few = hgf.at[h, rows_z(-2 * way, s * part_z, part_z)]
            copy(few, few, zg_send, zg.at[h, s, 3], (c, at_z(2 * way))).start()
            copy(own, own, zg_send, zg.at[h, s, 2], (c, at_z(way))).start()

    def z_came(h, i):
        for s in range(2):
            arrived(hgf.at[h, rows_z(2 * i * s - i)], zg.at[h, s, i - 1])

    def z_adam(h, i):
        adam(h, rows_z(i))
        adam(h, rows_z(-i))

    def z_end(h):
        for s in range(2):
            arrived(hgf.at[h, rows_z(far, s * part_z, part_z)], zg.at[h, s, 3])
        adam(h, rows_z(far))

    fh, fq = width // 2, width // 4

    def feats(t, lo, n):
        return pl.ds(t * fh + lo, n)

    def dest(t, du, dv):
        return PLACE[turned(t, du, dv)]

    def v_first(t, du):
        for s in range(2):
            src = part.at[dest(t, du, 2), k, feats(t, s * fq, fq)]
            to = dev(*turned(t, 0, 1 - 2 * s))
            copy(src, quart_in.at[t, du, s], rs_send, rs_q.at[t, du, s], to).start()

    def v_next(t, du):
        for s in range(2):
            arrived(quart_in.at[t, du, s], rs_q.at[t, du, s])
            to = dest(t, du, 1 - 2 * s)
            part[to, k, feats(t, s * fq, fq)] += quart_in[t, du, s]
            src = part.at[to, k, feats(t, 0, fh)]
            copy(src, half_in.at[t, du, s], rs_send, rs_h.at[t, du, s], dev(*turned(t, 0, 1 - 2 * s))).start()

    def v_last(t, du):
        to = dest(t, du, 0)
        for s in range(2):
            arrived(half_in.at[t, du, s], rs_h.at[t, du, s])
        total = part[to, k, feats(t, 0, fh)].astype(F32)
        total += half_in[t, du, 0].astype(F32) + half_in[t, du, 1].astype(F32)
        part[to, k, feats(t, 0, fh)] = total.astype(BF16)

    def u_first(t):
        for s in range(2):
            src = part.at[dest(t, 2, 0), k, feats(t, s * fq, fq)]
            copy(src, quart_in2.at[t, s], rs_send, rs_q2.at[t, s], dev(*turned(t, 1 - 2 * s, 0))).start()

    def u_next(t):
        for s in range(2):
            arrived(quart_in2.at[t, s], rs_q2.at[t, s])
            to = dest(t, 1 - 2 * s, 0)
            part[to, k, feats(t, s * fq, fq)] += quart_in2[t, s]
            src = part.at[to, k, feats(t, 0, fh)]
            copy(src, half_in2.at[t, s], rs_send, rs_h2.at[t, s], dev(*turned(t, 1 - 2 * s, 0))).start()

    def u_last(t):
        for s in range(2):
            arrived(half_in2.at[t, s], rs_h2.at[t, s])
        total = part[0, k, feats(t, 0, fh)].astype(F32)
        total += half_in2[t, 0].astype(F32) + half_in2[t, 1].astype(F32)
        egrad[:, t * fh : (t + 1) * fh] = total.T

    def g_first():
        gp[c // 2] = jnp.sum(wh[...].astype(F32) * hg[...], axis=0, keepdims=True) * 2.0

        def send(i, _):
            own = gp.at[c // 2]
            copy(own, own, g_send.at[0], g_recv.at[0], chip_peer(i)).start()
            return _

        lax.fori_loop(1, SIDE * SIDE, send, 0)

    def g_plane():
        arrived(gp.at[pl.ds(0, SIDE * SIDE - 1)], g_recv.at[0])
        gc[k] = jnp.sum(gp[...], axis=0)
        copy(gc.at[k], gc.at[k], g_send.at[1], g_recv.at[1], sibling).start()

    def g_z():
        arrived(gc.at[0], g_recv.at[1])
        gz[z] = gc[0] + gc[1]

        def send(i, _):
            copy(gz.at[z], gz.at[z], g_send.at[2], g_recv.at[2], (c, at_z(i))).start()
            return _

        lax.fori_loop(1, depth, send, 0)

    def g_last():
        arrived(gz.at[pl.ds(0, depth - 1)], g_recv.at[2])
        total = jnp.sum(gz[...], axis=0) / gain
        for i in range(width // 128):
            ggrad_ref[i : i + 1, :] = total[:, i * 128 : (i + 1) * 128]

    chunks = range(ZC)
    for h in chunks:
        gather_head(3, h * wide, wide)
        z_first(h)
    for t in range(2):
        v_first(t, 0)
    g_first()
    back(3)
    join(2)
    for h in chunks:
        z_second(h)
    join(3)
    for du in (2, 1, 3):
        for t in range(2):
            v_first(t, du)
    for t in range(2):
        v_next(t, 0)
    for h in chunks:
        z_third(h)
    for du in (2, 1):
        for t in range(2):
            v_next(t, du)
    g_plane()
    for t in range(2):
        v_next(t, 3)
    for h in chunks:
        z_last(h)
    g_z()
    loads[5].wait()
    loads[6].wait()
    for t in range(2):
        v_last(t, 2)
        u_first(t)
    for h in chunks:
        adam(h, rows_z(0))
    for h in chunks:
        z_spread(h)
    for t in range(2):
        v_last(t, 1)
    for t in range(2):
        v_last(t, 3)
    for t in range(2):
        u_next(t)
    for h in chunks:
        z_came(h, 1)
        z_adam(h, 1)
    for t in range(2):
        v_last(t, 0)
    for h in chunks:
        z_adam(h, 2)
    for h in chunks:
        z_came(h, 3)
        z_adam(h, 3)
    for t in range(2):
        u_last(t)

    scaled = egrad[...] * gain
    normed = normed_v[...]
    first_mean = jnp.mean(scaled, axis=1, keepdims=True)
    second_mean = jnp.mean(scaled * normed, axis=1, keepdims=True)
    igrad_ref[...] = ((scaled - first_mean - normed * second_mean) * inverse_v[...]).astype(BF16)

    g_last()
    for h in chunks:
        z_end(h)

    sent(emb.at[pl.ds(0, PLANE - 1)], ag_send)
    sent(from_core, core_send)
    sent(from_core.at[pl.ds(0, PLANE // 2 - 1)], rs_send)
    sent(ids.at[k, pl.ds(0, SIDE * SIDE - 1)], ids_send.at[0])
    sent(ids.at[k], ids_send.at[1])
    sent(gp.at[pl.ds(0, SIDE * SIDE - 1)], g_send.at[0])
    sent(gc.at[0], g_send.at[1])
    sent(gz.at[pl.ds(0, depth - 1)], g_send.at[2])
    sent(hgb.at[:, pl.ds(0, labels - piece)], z_send)
    sent(hgf.at[:, pl.ds(0, labels - piece)], zg_send)


def store(nh, nf, ns, igrad, ggrad, nh_out, nf_out, ns_out, igrad_out, ggrad_out, sem):
    pairs = ((nh, nh_out.at[0]), (nf, nf_out.at[0]), (ns, ns_out.at[0]), (igrad, igrad_out), (ggrad, ggrad_out))
    copies = [pltpu.make_async_copy(src, dst, sem.at[i]) for i, (src, dst) in enumerate(pairs)]
    for copy in copies:
        copy.start()
    for copy in copies:
        copy.wait()


def shards(
    hidden_states,
    ln_gain,
    beam_ids,
    positive_ids,
    cluster_sizes,
    head_rows,
    first_moment,
    second_moment,
):
    rows, width = hidden_states.shape
    labels = head_rows.shape[1]
    beam, pos = beam_ids.shape[1], positive_ids.shape[1]
    depth = lax.axis_size("dp")
    vmem = pl.BlockSpec(memory_space=pltpu.VMEM)
    hbm = pl.BlockSpec(memory_space=pltpu.HBM)
    fh, fq, piece, far, wide = width // 2, width // 4, labels // depth, depth // 2, width // ZC
    dma = pltpu.SemaphoreType.DMA
    head_shape = pltpu.VMEM((labels, width), F32)
    results = pl.pallas_call(
        kernel,
        out_shape=(
            head_shape,
            head_shape,
            head_shape,
            pltpu.VMEM((rows, width), BF16),
            pltpu.VMEM((width // 128, 128), F32),
        ),
        in_specs=[pl.BlockSpec(memory_space=pltpu.SMEM)] + [hbm] * 7,
        out_specs=(vmem,) * 5,
        scratch_shapes=[
            pltpu.VMEM((rows, width), BF16),
            pltpu.VMEM((width // 128, 128), F32),
            pltpu.VMEM((beam, rows), jnp.int32),
            pltpu.VMEM((pos, rows), jnp.int32),
            pltpu.VMEM((labels, width), F32),
            pltpu.VMEM((labels, width), F32),
            pltpu.VMEM((labels, width), F32),
            pltpu.VMEM((PLANE, rows, width), BF16),
            pltpu.VMEM((2, SIDE * SIDE, beam + pos, rows), jnp.int16),
            pltpu.VMEM((labels, width), BF16),
            pltpu.VMEM((width, labels), BF16),
            pltpu.VMEM((labels, width), F32),
            pltpu.VMEM((labels, 2 * MOST * rows), BF16),
            pltpu.VMEM((PLANE // 2, 2, width, rows), BF16),
            pltpu.VMEM((PLANE // 2, width, rows), BF16),
            pltpu.VMEM((2, SIDE, 2, fh, rows), BF16),
            pltpu.VMEM((2, SIDE, 2, fq, rows), BF16),
            pltpu.VMEM((2, 2, fh, rows), BF16),
            pltpu.VMEM((2, 2, fq, rows), BF16),
            pltpu.VMEM((ZC, labels, wide), BF16),
            pltpu.VMEM((ZC, labels, wide), BF16),
            pltpu.VMEM((ZC, 2, piece // 2, wide), BF16),
            pltpu.VMEM((ZC, 2, 3, piece, wide), BF16),
            pltpu.VMEM((SIDE * SIDE, 1, width), F32),
            pltpu.VMEM((2, 1, width), F32),
            pltpu.VMEM((depth, 1, width), F32),
            pltpu.VMEM((rows, width), F32),
            pltpu.VMEM((rows, width), F32),
            pltpu.VMEM((rows, 1), F32),
            dma((7,)),
            dma((2,)),
            dma((2,)),
            dma,
            dma((2, len(CHIPS))),
            dma((len(CHIPS),)),
            dma,
            dma((len(GROUPS),)),
            dma,
            dma((2, SIDE, 2)),
            dma((2, SIDE, 2)),
            dma((2, 2)),
            dma((2, 2)),
            dma,
            dma((ZC, 2)),
            dma((ZC, 2, 3)),
            dma,
            dma((ZC, 2, 4)),
            dma((3,)),
            dma((3,)),
        ],
        compiler_params=pltpu.CompilerParams(
            collective_id=0, has_side_effects=True, vmem_limit_bytes=48 * 1024 * 1024
        ),
    )(
        cluster_sizes,
        *(
            pltpu.with_memory_space_constraint(a, pltpu.HBM)
            for a in (
                hidden_states, ln_gain.reshape(width // 128, 128), beam_ids.T, positive_ids.T,
                head_rows[0], first_moment[0], second_moment[0],
            )
        ),
    )
    whole = pltpu.HBM((1, labels, width), F32)
    *rest, gain_grad = pl.pallas_call(
        store,
        out_shape=(whole, whole, whole, *[pltpu.HBM(r.shape, r.dtype) for r in results[3:]]),
        in_specs=[pl.BlockSpec(memory_space=pl.ANY)] * 5,
        out_specs=(hbm,) * 5,
        scratch_shapes=[dma((5,))],
        compiler_params=pltpu.CompilerParams(vmem_limit_bytes=16 * 1024 * 1024),
    )(*(pltpu.with_memory_space_constraint(r, pltpu.VMEM) for r in results))
    return (*rest, gain_grad.reshape(width))


def solution(mesh):
    in_specs = (
        P(("cluster", "dp"), None),
        P(),
        P(("cluster", "dp"), None),
        P(("cluster", "dp"), None),
        P("cluster"),
        P("cluster", None, None),
        P("cluster", None, None),
        P("cluster", None, None),
    )
    out_specs = (
        P("cluster", None, None),
        P("cluster", None, None),
        P("cluster", None, None),
        P(("cluster", "dp"), None),
        P(),
    )
    return jax.shard_map(shards, mesh=mesh, in_specs=in_specs, out_specs=out_specs, check_vma=False)
```

```python
import functools

import jax
import jax.numpy as jnp
from jax import lax
from jax.experimental import pallas as pl
from jax.experimental.pallas import tpu as pltpu
from jax.sharding import PartitionSpec as P

MESH = pl.DeviceIdType.MESH
F32 = jnp.float32
BF16 = jnp.bfloat16

norm_eps = 1e-05
learn_rate = 0.01
first_decay = 0.9
second_decay = 0.999
adam_eps = 1e-08
second_fix = 0.632304575226

SIDE = 4
PLANE = 32
CHIPS = (
    (0, 0), (1, 0), (0, 1), (3, 0), (0, 3), (2, 0), (0, 2), (1, 1),
    (3, 3), (1, 3), (3, 1), (2, 1), (1, 2), (2, 3), (3, 2), (2, 2),
)
PLACE = {offset: i for i, offset in enumerate(CHIPS)}
GROUPS = ((0, 5), (5, 3), (8, 3), (11, 5))
MOST = max(n for _, n in GROUPS)
ZC = 2


def kernel(
    size_in, hid_in, gain_in, beam_in, pos_in, head_in, first_in, second_in,
    nh_ref, nf_ref, ns_ref, igrad_ref, ggrad_ref,
    hid, gain_v, beam_v, pos_v, head, first, second,
    emb, ids, wh, wt, hg, slope_v, part, from_core, half_in, quart_in, half_in2, quart_in2,
    hgb, hgf, zq, zh, gp, gc, gz, egrad, normed_v, inverse_v,
    in_sem, ids_send, ids_recv, ag_send, ag_recv, core_recv,
    core_send, rs_core, rs_send, rs_h, rs_q, rs_h2, rs_q2,
    z_send, z_q, z_h, zg_send, zg, g_send, g_recv,
):
    c = lax.axis_index("cluster")
    z = lax.axis_index("dp")
    depth = lax.axis_size("dp")
    rows, width = hid.shape
    labels = head.shape[0]
    beam = beam_v.shape[0]
    x, y, k = c // (2 * SIDE), lax.rem(c // 2, SIDE), lax.rem(c, 2)
    sibling = (c + 1 - 2 * k, z)

    def dev(dx, dy):
        return ((lax.rem(x + dx, SIDE) * SIDE + lax.rem(y + dy, SIDE)) * 2 + k, z)

    def chip_peer(i):
        return (lax.rem(c // 2 + i, SIDE * SIDE) * 2 + k, z)

    def turned(t, du, dv):
        du, dv = du % SIDE, dv % SIDE
        return (du, dv) if t == 0 else (dv, du)

    def copy(src, dst, send, recv, device):
        return pltpu.make_async_remote_copy(
            src_ref=src, dst_ref=dst, send_sem=send, recv_sem=recv, device_id=device, device_id_type=MESH
        )

    def arrived(dst, recv):
        copy(dst, dst, recv, recv, sibling).wait_recv()

    def sent(src, send):
        copy(src, src, send, send, sibling).wait_send()

    loads = [
        pltpu.make_async_copy(src, dst, in_sem.at[i])
        for i, (src, dst) in enumerate(
            (
                (beam_in, beam_v), (pos_in, pos_v), (hid_in, hid), (gain_in, gain_v),
                (head_in, head), (first_in, first), (second_in, second),
            )
        )
    ]
    for load in loads:
        load.start()

    barrier = pltpu.get_barrier_semaphore()
    pl.semaphore_signal(barrier, inc=1, device_id=sibling, device_id_type=MESH)

    def greet_plane(i, _):
        pl.semaphore_signal(barrier, inc=1, device_id=chip_peer(i), device_id_type=MESH)
        return _

    def greet(i, _):
        pl.semaphore_signal(barrier, inc=1, device_id=(c, lax.rem(z + i, depth)), device_id_type=MESH)
        return _

    lax.fori_loop(1, SIDE * SIDE, greet_plane, 0)
    lax.fori_loop(1, depth, greet, 0)

    half, quart = rows // 2, rows // 4

    def push(t, at, lo, n, tu, tv):
        du, dv = turned(t, *CHIPS[at])
        to = PLACE[turned(t, du - tu, dv - tv)]
        src, dst = emb.at[2 * at + k, pl.ds(lo, n)], emb.at[2 * to + k, pl.ds(lo, n)]
        copy(src, dst, ag_send, ag_recv.at[t, to], dev(*turned(t, tu, tv))).start()

    def half_in_hand(t, du, dv, early=True, late=True):
        at, lo = PLACE[turned(t, du, dv)], t * half
        if at > 0 and early:
            arrived(emb.at[2 * at + k, pl.ds(lo, half)], ag_recv.at[t, at])
        if dv == 0:
            if not early:
                pass
            elif du == 0:
                push(t, at, lo, half, 1, 0)
                push(t, at, lo, half, -1, 0)
            elif du == 3:
                push(t, at, lo, quart, 1, 0)
            elif du == 1:
                push(t, at, lo + quart, quart, -1, 0)
            if late:
                push(t, at, lo, half, 0, 1)
                push(t, at, lo, half, 0, -1)
        elif dv == 3:
            push(t, at, lo, quart, 0, 1)
        elif dv == 1:
            push(t, at, lo + quart, quart, 0, -1)

    def event(*offsets, whole=()):
        for du, dv in offsets:
            for t in range(2):
                half_in_hand(t, du, dv)
        for offset in whole:
            mine = emb.at[2 * PLACE[offset] + k]
            copy(mine, mine, ag_send, core_recv.at[PLACE[offset]], sibling).start()

    for load in loads[:4]:
        load.wait()
    gain = jnp.concatenate([gain_v[i : i + 1, :] for i in range(width // 128)], axis=1)
    values = hid[...].astype(F32)
    center = jnp.mean(values, axis=1, keepdims=True)
    spread = jnp.mean(jnp.square(values - center), axis=1, keepdims=True)
    inverse = lax.rsqrt(spread + norm_eps)
    normed = (values - center) * inverse
    normed_v[...] = normed
    inverse_v[...] = inverse
    emb[k] = (normed * gain).astype(BF16)
    ids[k, c // 2] = jnp.concatenate([beam_v[...], pos_v[...]], axis=0).astype(jnp.int16)
    pl.semaphore_wait(barrier, SIDE * SIDE + depth - 1)

    def send_ids(i, _):
        own = ids.at[k, c // 2]
        copy(own, own, ids_send.at[0], ids_recv.at[0], chip_peer(i)).start()
        return _

    lax.fori_loop(1, SIDE * SIDE, send_ids, 0)
    event((0, 0), whole=((0, 0),))

    loads[4].wait()
    wh[...] = (head[...].astype(BF16) * 0.5).astype(BF16)
    for i in range(width // 128):
        cols = pl.ds(i * 128, 128)
        wt[cols, :] = head[:, cols].T.astype(BF16)
    hg[...] = jnp.zeros_like(hg)
    size = size_in[0]

    for early in (True, False):
        for du in (1, 3):
            for t in range(2):
                half_in_hand(t, du, 0, early, not early)
    arrived(ids.at[k, pl.ds(0, SIDE * SIDE - 1)], ids_recv.at[0])
    copy(ids.at[k], ids.at[k], ids_send.at[1], ids_recv.at[1], sibling).start()
    event((0, 1), (0, 3), whole=((1, 0), (0, 1), (3, 0), (0, 3)))
    def chips_of(g):
        first, n = GROUPS[g]
        return range(first, first + n)

    def block_of(g):
        first, n = GROUPS[g]
        return emb[pl.ds(2 * first, 2 * n)].reshape(2 * n * rows, width)

    def slope_of(g):
        return slope_v[:, : 2 * GROUPS[g][1] * rows]

    def score(g):
        label, limit = [], []
        many = 2 * GROUPS[g][1] * rows
        for at in chips_of(g):
            arrived(emb.at[2 * at + 1 - k], core_recv.at[at])
            dx, dy = CHIPS[at]
            for s in range(2):
                own = ids[s, lax.rem(x + dx, SIDE) * SIDE + lax.rem(y + dy, SIDE)].astype(jnp.int32)
                match = own[0:beam] == c
                place = lax.broadcasted_iota(jnp.int32, (beam, rows), 0)
                place = jnp.sum(jnp.where(match, place, 0), axis=0, keepdims=True)
                chosen = jnp.max(jnp.where(match, 1, 0), axis=0, keepdims=True)
                label.append(own[beam:] - place * labels)
                limit.append(chosen * size)
        label = jnp.concatenate(label, axis=1)
        limit = jnp.concatenate(limit, axis=1)
        logits = lax.dot_general(wh[...], block_of(g), (((1,), (1,)), ((), ())), preferred_element_type=F32)
        word = lax.shift_right_arithmetic(label, 5)
        bit = lax.shift_left(jnp.ones_like(label), label & 31)
        words = lax.broadcasted_iota(jnp.int32, (labels // 32, many), 0)
        bits = jnp.zeros_like(words)
        for p in range(label.shape[0]):
            bits = bits | jnp.where(word[p : p + 1] == words, bit[p : p + 1], 0)
        step = 0.5 / beam
        for i in range(labels // 32):
            slot = lax.broadcasted_iota(jnp.int32, (32, many), 0)
            hit = lax.shift_left(jnp.broadcast_to(bits[i : i + 1], (32, many)), 31 - slot) < 0
            slope = step * jnp.tanh(logits[32 * i : 32 * i + 32]) + jnp.where(hit, -step, step)
            slope = jnp.where(slot + 32 * i < limit, slope, 0.0)
            slope_v[pl.ds(32 * i, 32), :many] = slope.astype(BF16)

    def gather_head(g, lo=0, n=width):
        cols = pl.ds(lo, n)
        block = emb[pl.ds(2 * GROUPS[g][0], 2 * GROUPS[g][1]), :, cols].reshape(2 * GROUPS[g][1] * rows, n)
        hg[:, cols] += jnp.dot(slope_of(g), block, preferred_element_type=F32)

    def back(g):
        grads = jnp.dot(wt[...], slope_of(g), preferred_element_type=F32).astype(BF16)
        for q, at in enumerate(chips_of(g)):
            for s in range(2):
                i = 2 * q + s
                part[at, s] = grads[:, i * rows : (i + 1) * rows]
        there = pl.ds(*GROUPS[g])
        copy(part.at[there, 1 - k], from_core.at[there], core_send, rs_core.at[g], sibling).start()

    def join(g):
        arrived(from_core.at[pl.ds(*GROUPS[g])], rs_core.at[g])
        for at in chips_of(g):
            part[at, k] += from_core[at]

    arrived(ids.at[1 - k], ids_recv.at[1])
    score(0)
    gather_head(0)
    event((2, 0))
    back(0)
    event((1, 1), whole=((1, 1),))
    event((0, 2), whole=((2, 0), (0, 2)))
    score(1)
    event((3, 3), whole=((3, 3),))
    event((1, 3), (3, 1), whole=((1, 3), (3, 1)))
    gather_head(1)
    back(1)
    join(0)
    score(2)
    event((2, 1), (2, 3))
    gather_head(2)
    back(2)
    join(1)
    event((1, 2), (3, 2), whole=((2, 1), (1, 2), (2, 3), (3, 2)))
    event((2, 2), whole=((2, 2),))
    score(3)

    piece = labels // depth
    part_z = piece // 2
    far = depth // 2
    wide = width // ZC

    def at_z(i):
        return lax.rem(z + i + depth, depth)

    def rows_z(i, lo=0, n=piece):
        return pl.ds(pl.multiple_of(at_z(i) * piece + lo, part_z), n)

    def z_first(h):
        hgb[h] = hg[:, h * wide : (h + 1) * wide].astype(BF16)
        for s in range(2):
            way = 1 - 2 * s
            src = hgb.at[h, rows_z(far, s * part_z, part_z)]
            copy(src, zq.at[h, s], z_send, z_q.at[h, s], (c, at_z(way))).start()
        for s in range(2):
            way = 1 - 2 * s
            copy(hgb.at[h, rows_z(2 * way)], zh.at[h, s, 0], z_send, z_h.at[h, s, 0], (c, at_z(way))).start()

    def z_second(h):
        for s in range(2):
            way = 1 - 2 * s
            arrived(zq.at[h, s], z_q.at[h, s])
            hgb[h, rows_z(3 * way, s * part_z, part_z)] += zq[h, s]
            copy(hgb.at[h, rows_z(3 * way)], zh.at[h, s, 1], z_send, z_h.at[h, s, 1], (c, at_z(2 * way))).start()

    def z_third(h):
        for s in range(2):
            way = 1 - 2 * s
            arrived(zh.at[h, s, 0], z_h.at[h, s, 0])
            arrived(zh.at[h, s, 1], z_h.at[h, s, 1])
            total = hgb[h, rows_z(way)].astype(F32) + zh[h, s, 0].astype(F32) + zh[h, s, 1].astype(F32)
            hgb[h, rows_z(way)] = total.astype(BF16)
            copy(hgb.at[h, rows_z(way)], zh.at[h, s, 2], z_send, z_h.at[h, s, 2], (c, at_z(way))).start()

    def adam(h, at):
        cols = pl.ds(h * wide, wide)
        grad = hgf[h, at].astype(F32)
        new_first = first_decay * first[at, cols] + (1.0 - first_decay) * grad
        new_second = second_decay * second[at, cols] + (1.0 - second_decay) * grad * grad
        nf_ref[at, cols] = new_first
        ns_ref[at, cols] = new_second
        step_size = new_first / (jnp.sqrt(new_second * (1.0 / second_fix)) + adam_eps)
        nh_ref[at, cols] = head[at, cols] - learn_rate * step_size

    def z_last(h):
        total = hgb[h, rows_z(0)].astype(F32)
        for s in range(2):
            arrived(zh.at[h, s, 2], z_h.at[h, s, 2])
            total += zh[h, s, 2].astype(F32)
        hgf[h, rows_z(0)] = total.astype(BF16)
        own = hgf.at[h, rows_z(0)]
        for i in (2, 1):
            for s in range(2):
                copy(own, own, zg_send, zg.at[h, s, i - 1], (c, at_z(i - 2 * i * s))).start()

    def z_spread(h):
        for s in range(2):
            way = 1 - 2 * s
            own = hgf.at[h, rows_z(-2 * way)]
            arrived(own, zg.at[h, s, 1])
            few = hgf.at[h, rows_z(-2 * way, s * part_z, part_z)]
            copy(few, few, zg_send, zg.at[h, s, 3], (c, at_z(2 * way))).start()
            copy(own, own, zg_send, zg.at[h, s, 2], (c, at_z(way))).start()

    def z_came(h, i):
        for s in range(2):
            arrived(hgf.at[h, rows_z(2 * i * s - i)], zg.at[h, s, i - 1])

    def z_adam(h, i):
        adam(h, rows_z(i))
        adam(h, rows_z(-i))

    def z_end(h):
        for s in range(2):
            arrived(hgf.at[h, rows_z(far, s * part_z, part_z)], zg.at[h, s, 3])
        adam(h, rows_z(far))

    fh, fq = width // 2, width // 4

    def feats(t, lo, n):
        return pl.ds(t * fh + lo, n)

    def dest(t, du, dv):
        return PLACE[turned(t, du, dv)]

    def v_first(t, du):
        for s in range(2):
            src = part.at[dest(t, du, 2), k, feats(t, s * fq, fq)]
            to = dev(*turned(t, 0, 1 - 2 * s))
            copy(src, quart_in.at[t, du, s], rs_send, rs_q.at[t, du, s], to).start()

    def v_next(t, du):
        for s in range(2):
            arrived(quart_in.at[t, du, s], rs_q.at[t, du, s])
            to = dest(t, du, 1 - 2 * s)
            part[to, k, feats(t, s * fq, fq)] += quart_in[t, du, s]
            src = part.at[to, k, feats(t, 0, fh)]
            copy(src, half_in.at[t, du, s], rs_send, rs_h.at[t, du, s], dev(*turned(t, 0, 1 - 2 * s))).start()

    def v_last(t, du):
        to = dest(t, du, 0)
        for s in range(2):
            arrived(half_in.at[t, du, s], rs_h.at[t, du, s])
        total = part[to, k, feats(t, 0, fh)].astype(F32)
        total += half_in[t, du, 0].astype(F32) + half_in[t, du, 1].astype(F32)
        part[to, k, feats(t, 0, fh)] = total.astype(BF16)

    def u_first(t):
        for s in range(2):
            src = part.at[dest(t, 2, 0), k, feats(t, s * fq, fq)]
            copy(src, quart_in2.at[t, s], rs_send, rs_q2.at[t, s], dev(*turned(t, 1 - 2 * s, 0))).start()

    def u_next(t):
        for s in range(2):
            arrived(quart_in2.at[t, s], rs_q2.at[t, s])
            to = dest(t, 1 - 2 * s, 0)
            part[to, k, feats(t, s * fq, fq)] += quart_in2[t, s]
            src = part.at[to, k, feats(t, 0, fh)]
            copy(src, half_in2.at[t, s], rs_send, rs_h2.at[t, s], dev(*turned(t, 1 - 2 * s, 0))).start()

    def u_last(t):
        for s in range(2):
            arrived(half_in2.at[t, s], rs_h2.at[t, s])
        total = part[0, k, feats(t, 0, fh)].astype(F32)
        total += half_in2[t, 0].astype(F32) + half_in2[t, 1].astype(F32)
        egrad[:, t * fh : (t + 1) * fh] = total.T

    def g_first():
        gp[c // 2] = jnp.sum(wh[...].astype(F32) * hg[...], axis=0, keepdims=True) * 2.0

        def send(i, _):
            own = gp.at[c // 2]
            copy(own, own, g_send.at[0], g_recv.at[0], chip_peer(i)).start()
            return _

        lax.fori_loop(1, SIDE * SIDE, send, 0)

    def g_plane():
        arrived(gp.at[pl.ds(0, SIDE * SIDE - 1)], g_recv.at[0])
        gc[k] = jnp.sum(gp[...], axis=0)
        copy(gc.at[k], gc.at[k], g_send.at[1], g_recv.at[1], sibling).start()

    def g_z():
        arrived(gc.at[0], g_recv.at[1])
        gz[z] = gc[0] + gc[1]

        def send(i, _):
            copy(gz.at[z], gz.at[z], g_send.at[2], g_recv.at[2], (c, at_z(i))).start()
            return _

        lax.fori_loop(1, depth, send, 0)

    def g_last():
        arrived(gz.at[pl.ds(0, depth - 1)], g_recv.at[2])
        total = jnp.sum(gz[...], axis=0) / gain
        for i in range(width // 128):
            ggrad_ref[i : i + 1, :] = total[:, i * 128 : (i + 1) * 128]

    chunks = range(ZC)
    for h in chunks:
        gather_head(3, h * wide, wide)
        z_first(h)
    for t in range(2):
        v_first(t, 0)
    g_first()
    back(3)
    for h in chunks:
        z_second(h)
    join(2)
    join(3)
    for du in (2, 1, 3):
        for t in range(2):
            v_first(t, du)
    for t in range(2):
        v_next(t, 0)
    for h in chunks:
        z_third(h)
    for du in (2, 1):
        for t in range(2):
            v_next(t, du)
    g_plane()
    for t in range(2):
        v_next(t, 3)
    for h in chunks:
        z_last(h)
    g_z()
    loads[5].wait()
    loads[6].wait()
    for t in range(2):
        v_last(t, 2)
        u_first(t)
    for h in chunks:
        adam(h, rows_z(0))
    for h in chunks:
        z_spread(h)
    for t in range(2):
        v_last(t, 1)
    for t in range(2):
        v_last(t, 3)
    for t in range(2):
        u_next(t)
    for h in chunks:
        z_came(h, 1)
        z_adam(h, 1)
    for t in range(2):
        v_last(t, 0)
    for h in chunks:
        z_adam(h, 2)
    for h in chunks:
        z_came(h, 3)
        z_adam(h, 3)
    for t in range(2):
        u_last(t)

    scaled = egrad[...] * gain
    normed = normed_v[...]
    first_mean = jnp.mean(scaled, axis=1, keepdims=True)
    second_mean = jnp.mean(scaled * normed, axis=1, keepdims=True)
    igrad_ref[...] = ((scaled - first_mean - normed * second_mean) * inverse_v[...]).astype(BF16)

    g_last()
    for h in chunks:
        z_end(h)

    sent(emb.at[pl.ds(0, PLANE - 1)], ag_send)
    sent(from_core, core_send)
    sent(from_core.at[pl.ds(0, PLANE // 2 - 1)], rs_send)
    sent(ids.at[k, pl.ds(0, SIDE * SIDE - 1)], ids_send.at[0])
    sent(ids.at[k], ids_send.at[1])
    sent(gp.at[pl.ds(0, SIDE * SIDE - 1)], g_send.at[0])
    sent(gc.at[0], g_send.at[1])
    sent(gz.at[pl.ds(0, depth - 1)], g_send.at[2])
    sent(hgb.at[:, pl.ds(0, labels - piece)], z_send)
    sent(hgf.at[:, pl.ds(0, labels - piece)], zg_send)


def store(nh, nf, ns, igrad, ggrad, nh_out, nf_out, ns_out, igrad_out, ggrad_out, sem):
    pairs = ((nh, nh_out.at[0]), (nf, nf_out.at[0]), (ns, ns_out.at[0]), (igrad, igrad_out), (ggrad, ggrad_out))
    copies = [pltpu.make_async_copy(src, dst, sem.at[i]) for i, (src, dst) in enumerate(pairs)]
    for copy in copies:
        copy.start()
    for copy in copies:
        copy.wait()


def shards(
    hidden_states,
    ln_gain,
    beam_ids,
    positive_ids,
    cluster_sizes,
    head_rows,
    first_moment,
    second_moment,
):
    rows, width = hidden_states.shape
    labels = head_rows.shape[1]
    beam, pos = beam_ids.shape[1], positive_ids.shape[1]
    depth = lax.axis_size("dp")
    vmem = pl.BlockSpec(memory_space=pltpu.VMEM)
    hbm = pl.BlockSpec(memory_space=pltpu.HBM)
    fh, fq, piece, far, wide = width // 2, width // 4, labels // depth, depth // 2, width // ZC
    dma = pltpu.SemaphoreType.DMA
    head_shape = pltpu.VMEM((labels, width), F32)
    results = pl.pallas_call(
        kernel,
        out_shape=(
            head_shape,
            head_shape,
            head_shape,
            pltpu.VMEM((rows, width), BF16),
            pltpu.VMEM((width // 128, 128), F32),
        ),
        in_specs=[pl.BlockSpec(memory_space=pltpu.SMEM)] + [hbm] * 7,
        out_specs=(vmem,) * 5,
        scratch_shapes=[
            pltpu.VMEM((rows, width), BF16),
            pltpu.VMEM((width // 128, 128), F32),
            pltpu.VMEM((beam, rows), jnp.int32),
            pltpu.VMEM((pos, rows), jnp.int32),
            pltpu.VMEM((labels, width), F32),
            pltpu.VMEM((labels, width), F32),
            pltpu.VMEM((labels, width), F32),
            pltpu.VMEM((PLANE, rows, width), BF16),
            pltpu.VMEM((2, SIDE * SIDE, beam + pos, rows), jnp.int16),
            pltpu.VMEM((labels, width), BF16),
            pltpu.VMEM((width, labels), BF16),
            pltpu.VMEM((labels, width), F32),
            pltpu.VMEM((labels, 2 * MOST * rows), BF16),
            pltpu.VMEM((PLANE // 2, 2, width, rows), BF16),
            pltpu.VMEM((PLANE // 2, width, rows), BF16),
            pltpu.VMEM((2, SIDE, 2, fh, rows), BF16),
            pltpu.VMEM((2, SIDE, 2, fq, rows), BF16),
            pltpu.VMEM((2, 2, fh, rows), BF16),
            pltpu.VMEM((2, 2, fq, rows), BF16),
            pltpu.VMEM((ZC, labels, wide), BF16),
            pltpu.VMEM((ZC, labels, wide), BF16),
            pltpu.VMEM((ZC, 2, piece // 2, wide), BF16),
            pltpu.VMEM((ZC, 2, 3, piece, wide), BF16),
            pltpu.VMEM((SIDE * SIDE, 1, width), F32),
            pltpu.VMEM((2, 1, width), F32),
            pltpu.VMEM((depth, 1, width), F32),
            pltpu.VMEM((rows, width), F32),
            pltpu.VMEM((rows, width), F32),
            pltpu.VMEM((rows, 1), F32),
            dma((7,)),
            dma((2,)),
            dma((2,)),
            dma,
            dma((2, len(CHIPS))),
            dma((len(CHIPS),)),
            dma,
            dma((len(GROUPS),)),
            dma,
            dma((2, SIDE, 2)),
            dma((2, SIDE, 2)),
            dma((2, 2)),
            dma((2, 2)),
            dma,
            dma((ZC, 2)),
            dma((ZC, 2, 3)),
            dma,
            dma((ZC, 2, 4)),
            dma((3,)),
            dma((3,)),
        ],
        compiler_params=pltpu.CompilerParams(
            collective_id=0, has_side_effects=True, vmem_limit_bytes=48 * 1024 * 1024
        ),
    )(
        cluster_sizes,
        *(
            pltpu.with_memory_space_constraint(a, pltpu.HBM)
            for a in (
                hidden_states, ln_gain.reshape(width // 128, 128), beam_ids.T, positive_ids.T,
                head_rows[0], first_moment[0], second_moment[0],
            )
        ),
    )
    whole = pltpu.HBM((1, labels, width), F32)
    *rest, gain_grad = pl.pallas_call(
        store,
        out_shape=(whole, whole, whole, *[pltpu.HBM(r.shape, r.dtype) for r in results[3:]]),
        in_specs=[pl.BlockSpec(memory_space=pl.ANY)] * 5,
        out_specs=(hbm,) * 5,
        scratch_shapes=[dma((5,))],
        compiler_params=pltpu.CompilerParams(vmem_limit_bytes=16 * 1024 * 1024),
    )(*(pltpu.with_memory_space_constraint(r, pltpu.VMEM) for r in results))
    return (*rest, gain_grad.reshape(width))


def solution(mesh):
    in_specs = (
        P(("cluster", "dp"), None),
        P(),
        P(("cluster", "dp"), None),
        P(("cluster", "dp"), None),
        P("cluster"),
        P("cluster", None, None),
        P("cluster", None, None),
        P("cluster", None, None),
    )
    out_specs = (
        P("cluster", None, None),
        P("cluster", None, None),
        P("cluster", None, None),
        P(("cluster", "dp"), None),
        P(),
    )
    return jax.shard_map(shards, mesh=mesh, in_specs=in_specs, out_specs=out_specs, check_vma=False)
```
